256 devices in a mesh: row: 8 (over y, core), col: 32 (over z, x).
Axes of the slice: x: 4, y: 4, z: 8, core: 2. Of those that a mesh axis runs over, the one named last changes fastest.
Arguments:
- layer_input: bfloat16 [512, 8192], P('row', 'col'), may hold values from -36 to 36, as said below
- norm_gain: float32 [8192], P('col'), may hold values from 0.1 to 1.9
- w_gate: bfloat16 [8192, 14336], P('col', 'row'), may hold values from -0.09375 to 0.09375
- w_up: bfloat16 [8192, 14336], P('col', 'row'), may hold values from -0.09375 to 0.09375
- w_down: bfloat16 [14336, 8192], P('row', 'col'), may hold values from -0.09375 to 0.09375
- mask_gate: int32 [64, 112], P('col', 'row'), may hold values 0 or 1
- mask_up: int32 [64, 112], P('col', 'row'), may hold values 0 or 1
- mask_down: int32 [112, 64], P('row', 'col'), may hold values 0 or 1
- out_grad: bfloat16 [512, 8192], P('row', 'col'), may hold values from -6 to 6
Outputs:
- layer_out: bfloat16 [512, 8192], P('row', 'col')
- input_grad: bfloat16 [512, 8192], P('row', 'col')
- gain_grad: float32 [8192], P('col')
- gate_wgrad: bfloat16 [8192, 14336], P('col', 'row')
- up_wgrad: bfloat16 [8192, 14336], P('col', 'row')
- down_wgrad: bfloat16 [14336, 8192], P('row', 'col')
The draws below stay inside these ranges and needn't reach their ends.
Inputs may be any that keep to these rules, and one draw needn't show every extreme that they name: `layer_input`: the layer input's rows and features have scales that differ by up to a factor of ten.
All inputs are finite; a program needn't handle non-finite values. No bound on the sum of `mask_gate` or of `mask_up` or of `mask_down` on one device may be relied on, other than what follows from the above.
Results may differ from the reference program's by a relative error of at most 0.02.
Values may be sent and summed in bfloat16 or wider, within the bound.
No kernel may reach another device: no remote copies, remote signals or barrier semaphores. Data moves between devices by JAX's collectives and lax.ppermute only.
A program may use at most 192 MiB of HBM per device.

```python
import math
import jax
import jax.numpy as jnp
from jax import lax

D = 8192
FF = 14336
BLK = 128
TOKENS = 512


def draw_layer_input(key, part):
    row_key = jax.random.fold_in(key, 11)
    col_key = jax.random.fold_in(key, 12)
    base_key = jax.random.fold_in(key, 13)
    row_scale = jnp.exp(jax.random.uniform(row_key, (TOKENS, 1), jnp.float32, math.log(0.3), math.log(3.0)))
    col_scale = jnp.exp(jax.random.uniform(col_key, (1, D), jnp.float32, math.log(0.3), math.log(3.0)))
    base = jax.random.truncated_normal(base_key, -4.0, 4.0, (TOKENS, D), jnp.float32)
    return (base * row_scale * col_scale).astype(jnp.bfloat16)


def place_ends(array, key, smallest, largest):
    longest = array.shape.index(max(array.shape))
    spots = []
    for shift in (0, 1):
        where = [jax.random.randint(jax.random.fold_in(key, axis), (), 0, length) for axis, length in enumerate(array.shape)]
        where[longest] = (where[longest] + shift) % array.shape[longest]
        spots.append(tuple(where))
    return array.at[spots[0]].set(smallest).at[spots[1]].set(largest)


def shard_levels(stream_key, shape, split, least, largest):
    def one(dim, blocks):
        draws = jax.random.uniform(jax.random.fold_in(jax.random.fold_in(stream_key, 6), dim), (blocks,), jnp.float32, least / len(split), largest / len(split))
        return jnp.repeat(jnp.exp(draws), shape[dim] // blocks).reshape((-1,) + (1,) * (len(shape) - dim - 1))

    gain = one(*split[0])
    for cut in split[1:]:
        gain = gain * one(*cut)
    return gain


def gaussian(rng, extent, scale, limit, pieces=(), held_as=jnp.bfloat16):
    factor_of = shard_levels(rng, extent, pieces, -0.22, 0.18) if pieces else 1.0
    drawn = jax.random.normal(rng, extent, jnp.float32) * scale * factor_of
    return jnp.minimum(jnp.maximum(drawn, -limit), limit).astype(held_as)


def setup_inputs(seed: int = 0) -> dict:
    splits = jax.random.split(jax.random.key(seed), 10)
    layer_input = draw_layer_input(jax.random.fold_in(splits[9], 71), 0)
    norm_gain = jnp.clip(1.0 + 0.18 * jax.random.normal(splits[1], (D,), jnp.float32), 0.1, 1.9)
    w_gate = gaussian(splits[2], (D, FF), (D // 2) ** -0.5, 0.09375, ((0, 32), (1, 8)))
    w_up = gaussian(splits[3], (D, FF), (D // 2) ** -0.5, 0.09375, ((0, 32), (1, 8)))
    w_down = gaussian(splits[4], (FF, D), (FF // 4) ** -0.5, 0.09375, ((0, 8), (1, 32)))
    mask_gate = place_ends((jax.random.randint(splits[5], (D // BLK, FF // BLK), 0, 2) < 1).astype(jnp.int32), jax.random.fold_in(splits[5], 1), 0, 1)
    mask_up = place_ends((jax.random.randint(splits[6], (D // BLK, FF // BLK), 0, 2) < 1).astype(jnp.int32), jax.random.fold_in(splits[6], 1), 0, 1)
    mask_down = place_ends((jax.random.randint(splits[7], (FF // BLK, D // BLK), 0, 2) < 1).astype(jnp.int32), jax.random.fold_in(splits[7], 1), 0, 1)
    out_grad = gaussian(splits[8], (TOKENS, D), 1.0, 6.0, ((0, 8), (1, 32)))
    return dict(layer_input=layer_input, norm_gain=norm_gain, w_gate=w_gate, w_up=w_up, w_down=w_down, mask_gate=mask_gate, mask_up=mask_up, mask_down=mask_down, out_grad=out_grad)


norm_eps = 1e-05

def apply_mask(weight, mask):
    block_rows, block_cols = mask.shape
    row_count, col_count = weight.shape
    blocks = weight.reshape(block_rows, row_count // block_rows, block_cols, col_count // block_cols)
    keep = mask.astype(weight.dtype)[:, None, :, None]
    return (blocks * keep).reshape(row_count, col_count)

def contract_rows(left, right):
    return lax.dot_general(left, right, (((0,), (0,)), ((), ())), preferred_element_type=jnp.float32)

def contract_cols(left, right):
    return lax.dot_general(left, right, (((1,), (1,)), ((), ())), preferred_element_type=jnp.float32)

def reference(layer_input, norm_gain, w_gate, w_up, w_down, mask_gate, mask_up, mask_down, out_grad):
    x_float = layer_input.astype(jnp.float32)
    scale = lax.rsqrt(lax.optimization_barrier(jnp.sum(x_float * x_float, axis=1)) / D + norm_eps)[:, None]
    normed = (x_float * scale * norm_gain[None, :]).astype(jnp.bfloat16)
    eff_gate = apply_mask(w_gate, mask_gate)
    eff_up = apply_mask(w_up, mask_up)
    eff_down = apply_mask(w_down, mask_down)
    gate = jnp.dot(normed, eff_gate, preferred_element_type=jnp.float32)
    up = jnp.dot(normed, eff_up, preferred_element_type=jnp.float32)
    act = (jax.nn.silu(gate) * up).astype(jnp.bfloat16)
    layer_out = (x_float + jnp.dot(act, eff_down, preferred_element_type=jnp.float32)).astype(jnp.bfloat16)
    act_grad = contract_cols(out_grad, eff_down)
    down_wgrad = apply_mask(contract_rows(act, out_grad), mask_down).astype(jnp.bfloat16)
    sig = jax.nn.sigmoid(gate)
    gate_grad = (act_grad * up * sig * (1.0 + gate * (1.0 - sig))).astype(jnp.bfloat16)
    up_grad = (act_grad * gate * sig).astype(jnp.bfloat16)
    gate_wgrad = apply_mask(contract_rows(normed, gate_grad), mask_gate).astype(jnp.bfloat16)
    up_wgrad = apply_mask(contract_rows(normed, up_grad), mask_up).astype(jnp.bfloat16)
    normed_grad = contract_cols(gate_grad, eff_gate) + contract_cols(up_grad, eff_up)
    gain_grad = lax.optimization_barrier(jnp.sum(normed_grad * x_float * scale, axis=0))
    dots = lax.optimization_barrier(jnp.sum(normed_grad * norm_gain[None, :] * x_float, axis=1))[:, None]
    input_grad = (out_grad.astype(jnp.float32) + scale * norm_gain[None, :] * normed_grad - x_float * scale * scale * scale * dots / D).astype(jnp.bfloat16)
    return (layer_out, input_grad, gain_grad, gate_wgrad, up_wgrad, down_wgrad)
```

```python
import jax
import jax.numpy as jnp
from jax import lax
from jax.experimental import pallas as pl
from jax.experimental.pallas import tpu as pltpu
from jax.sharding import Mesh
from jax.sharding import PartitionSpec as P

D = 8192
BLK = 128
NZ, NX = 8, 4
COL = ("col_0", "col_1")
ALL = ("row", "col_0", "col_1")
norm_eps = 1e-05

f32 = jnp.float32
bf16 = jnp.bfloat16
VMEM_BYTES = 56 * 1024 * 1024


def vmem():
    return pl.BlockSpec(memory_space=pltpu.VMEM)


def smem():
    return pl.BlockSpec(memory_space=pltpu.SMEM)


def call(kernel, outs, in_specs, scratch, flops, nbytes, args):
    return pl.pallas_call(
        kernel,
        out_shape=outs,
        in_specs=in_specs,
        out_specs=tuple(vmem() for _ in outs),
        scratch_shapes=scratch,
        compiler_params=pltpu.CompilerParams(vmem_limit_bytes=VMEM_BYTES),
        cost_estimate=pl.CostEstimate(flops=flops, bytes_accessed=nbytes, transcendentals=0),
    )(*args)


def natural_row(pos, k, j):
    return pl.multiple_of(
        lax.rem(pos[0] + k, NZ) * (NX * 16) + lax.rem(pos[1] + j, NX) * 16, 16
    )


def nn(a, b):
    return jnp.dot(a, b, preferred_element_type=f32)


def nt(a, b):
    return lax.dot_general(a, b, (((1,), (1,)), ((), ())), preferred_element_type=f32)


def tn(a, b):
    return lax.dot_general(a, b, (((0,), (0,)), ((), ())), preferred_element_type=f32)


def partials_kernel(
    pos, mg, mu, md, rows, gain, wg, wu, wd, part_a, part_b, eff_g, eff_u, eff_d, la, lb
):
    for w, m, e in ((wg, mg, eff_g), (wu, mu, eff_u), (wd, md, eff_d)):
        for a in range(w.shape[0] // BLK):
            for b in range(w.shape[1] // BLK):
                r, c = slice(a * BLK, (a + 1) * BLK), slice(b * BLK, (b + 1) * BLK)
                e[r, c] = w[r, c] * m[a, b].astype(f32).astype(bf16)
    width = gain.shape[1]
    for k in range(NZ):
        for j in range(NX):
            at = pl.ds(natural_row(pos, k, j), 16)
            to_a = slice((j * NZ + k) * 16, (j * NZ + k) * 16 + 16)
            to_b = slice((k * NX + j) * 16, (k * NX + j) * 16 + 16)
            x = (rows[at, :width].astype(f32) * gain[...]).astype(bf16)
            g = rows[at, width:]
            la[to_a, :width] = x
            lb[to_b, :width] = x
            la[to_a, width:] = g
            lb[to_b, width:] = g
    half = wg.shape[1] // 2
    for left, part, at in ((lb, part_b, half), (la, part_a, 0)):
        cols = slice(at, at + half)
        for t in range(0, left.shape[0], 128):
            tok = slice(t, t + 128)
            x, g = left[tok, :width], left[tok, width:]
            part[tok, :half] = nn(x, eff_g[:, cols]).astype(bf16)
            part[tok, half : 2 * half] = nn(x, eff_u[:, cols]).astype(bf16)
            part[tok, 2 * half :] = nt(g, eff_d[cols, :]).astype(bf16)


def features_kernel(
    pos, rows, scale, ga, gb, eff_g, eff_u, eff_d, both, gain_part, da, na, db, nb
):
    half = ga.shape[1] // 3
    width = eff_g.shape[0]
    for hid, d, n, at in ((ga, da, na, 0), (gb, db, nb, half)):
        cols = slice(at, at + half)
        for t in range(0, hid.shape[0], 128):
            tok = slice(t, t + 128)
            d[tok, :] = nn(hid[tok, :half], eff_d[cols, :])
            n[tok, :] = nt(hid[tok, half : 2 * half], eff_g[:, cols]) + nt(
                hid[tok, 2 * half :], eff_u[:, cols]
            )
    total = jnp.zeros((16, width), f32)
    for k in range(NZ):
        for j in range(NX):
            at = pl.ds(natural_row(pos, k, j), 16)
            in_a = slice((j * NZ + k) * 16, (j * NZ + k) * 16 + 16)
            in_b = slice((k * NX + j) * 16, (k * NX + j) * 16 + 16)
            both[at, :width] = (da[in_a, :] + db[in_b, :]).astype(bf16)
            grad = na[in_a, :] + nb[in_b, :]
            both[at, width:] = grad.astype(bf16)
            total += grad * rows[at, :width].astype(f32) * scale[at, :]
    gain_part[...] = jnp.sum(total, axis=0, keepdims=True)


def weights_kernel(
    pos, mg, mu, md, rows, gain, scale, ga, gb, out_g, out_u, out_d, la, lb
):
    width = gain.shape[1]
    for k in range(NZ):
        for j in range(NX):
            at = pl.ds(natural_row(pos, k, j), 16)
            to_a = slice((j * NZ + k) * 16, (j * NZ + k) * 16 + 16)
            to_b = slice((k * NX + j) * 16, (k * NX + j) * 16 + 16)
            x = (rows[at, :width].astype(f32) * scale[at, :] * gain[...]).astype(bf16)
            g = rows[at, width:]
            la[to_a, :width] = x
            lb[to_b, :width] = x
            la[to_a, width:] = g
            lb[to_b, width:] = g
    half = ga.shape[1] // 3
    for hid, left, at in ((ga, la, 0), (gb, lb, half)):
        normed, grad = left[:, :width], left[:, width:]
        for c in range(0, half, BLK):
            b = (at + c) // BLK
            gw = tn(normed, hid[:, half + c : half + c + BLK])
            uw = tn(normed, hid[:, 2 * half + c : 2 * half + c + BLK])
            dw = tn(hid[:, c : c + BLK], grad)
            to = slice(at + c, at + c + BLK)
            for a in range(width // BLK):
                r = slice(a * BLK, (a + 1) * BLK)
                out_g[r, to] = (gw[r, :] * mg[a, b].astype(f32)).astype(bf16)
                out_u[r, to] = (uw[r, :] * mu[a, b].astype(f32)).astype(bf16)
                out_d[to, r] = (dw[:, r] * md[b, a].astype(f32)).astype(bf16)


def send(v, axis, step):
    n = lax.axis_size(axis)
    return lax.ppermute(v, axis, [(i, (i + step) % n) for i in range(n)])


def up32(v):
    return v.astype(f32)


def add_top(piece, got, h):
    return jnp.concatenate([(up32(piece[:h]) + up32(got)).astype(bf16), piece[h:].astype(bf16)])


def add_bottom(piece, got, h):
    return jnp.concatenate([piece[:h].astype(bf16), (up32(piece[h:]) + up32(got)).astype(bf16)])


def plus(piece, got):
    return (up32(piece) + up32(got)).astype(bf16)


def reduce_ring(pieces, axis):
    n = len(pieces)
    far = pieces[n // 2].astype(bf16)
    h = far.shape[0] // 2
    right, left = send(far[:h], axis, 1), send(far[h:], axis, -1)
    for away in range(n // 2 - 1, 0, -1):
        to_right, to_left = pieces[away], pieces[n - away]
        if away == n // 2 - 1:
            right = send(add_top(to_right, right, h), axis, 1)
            left = send(add_bottom(to_left, left, h), axis, -1)
        else:
            right = send(plus(to_right, right), axis, 1)
            left = send(plus(to_left, left), axis, -1)
    return up32(pieces[0]) + up32(right) + up32(left)


def gather_ring(shard, axis):
    n = lax.axis_size(axis)
    h = shard.shape[0] // 2
    pieces = [None] * n
    pieces[0] = shard
    right = left = shard
    for away in range(1, n // 2):
        right, left = send(right, axis, 1), send(left, axis, -1)
        pieces[n - away], pieces[away] = right, left
    pieces[n // 2] = jnp.concatenate([send(right[:h], axis, 1), send(left[h:], axis, -1)])
    return jnp.concatenate(pieces)


def cut(v, n):
    m = v.shape[0] // n
    return [v[i * m : (i + 1) * m] for i in range(n)]


def hidden_grads(sums, scale):
    half = sums.shape[1] // 3
    gate, up = sums[:, :half] * scale, sums[:, half : 2 * half] * scale
    act_grad = sums[:, 2 * half :]
    sig = jax.nn.sigmoid(gate)
    act = (gate * sig * up).astype(bf16)
    gate_grad = (act_grad * up * sig * (1.0 + gate * (1.0 - sig))).astype(bf16)
    up_grad = (act_grad * gate * sig).astype(bf16)
    dots = jnp.sum(up32(gate_grad) * gate + up32(up_grad) * up, axis=1)
    return jnp.concatenate([act, gate_grad, up_grad], axis=1), dots


def from_everyone(shard, axis):
    copies = jnp.broadcast_to(shard, (lax.axis_size(axis), *shard.shape))
    return lax.all_to_all(copies, axis, split_axis=0, concat_axis=0, tiled=True)


def shards(layer_input, norm_gain, w_gate, w_up, w_down, mask_gate, mask_up, mask_down, out_grad):
    row, z, x = (lax.axis_index(a) for a in ALL)
    pos = jnp.stack([z, x]).astype(jnp.int32)
    gain = norm_gain[None, :]
    mine, width = layer_input.shape
    hidden = w_gate.shape[1]
    rows = from_everyone(jnp.concatenate([layer_input, out_grad], axis=1), "row")
    rows = rows.reshape(-1, 2 * width)
    tokens = rows.shape[0]
    wide = 3 * hidden // 2
    part = jax.ShapeDtypeStruct((tokens, wide), bf16)
    dots_flops = 2 * tokens * width * hidden * 3
    part_a, part_b, eff_gate, eff_up, eff_down = call(
        partials_kernel,
        (
            part,
            part,
            jax.ShapeDtypeStruct(w_gate.shape, bf16),
            jax.ShapeDtypeStruct(w_up.shape, bf16),
            jax.ShapeDtypeStruct(w_down.shape, bf16),
        ),
        [smem()] * 4 + [vmem()] * 5,
        [pltpu.VMEM((tokens, 2 * width), bf16)] * 2,
        dots_flops,
        12_000_000,
        (pos, mask_gate, mask_up, mask_down, rows, gain, w_gate, w_up, w_down),
    )
    squares = jnp.sum(jnp.square(up32(rows[:, :width])), axis=1)
    scale_all = lax.rsqrt(lax.psum(squares, COL) / D + norm_eps)[:, None]

    sums_b = reduce_ring(cut(reduce_ring(cut(part_b, NZ), "col_0"), NX), "col_1")
    sums_a = reduce_ring(cut(reduce_ring(cut(part_a, NX), "col_1"), NZ), "col_0")
    own = z * (NX * 16) + x * 16
    scale_own = lax.dynamic_slice_in_dim(scale_all, own, 16, 0)
    hid_a, dots_a = hidden_grads(sums_a, scale_own)
    hid_b, dots_b = hidden_grads(sums_b, scale_own)
    dots_all = lax.psum(
        lax.dynamic_update_slice_in_dim(jnp.zeros((tokens,), f32), dots_a + dots_b, own, 0), ALL
    )
    all_a = gather_ring(gather_ring(hid_a, "col_0"), "col_1")
    all_b = gather_ring(gather_ring(hid_b, "col_1"), "col_0")

    both, gain_part = call(
        features_kernel,
        (
            jax.ShapeDtypeStruct((tokens, 2 * width), bf16),
            jax.ShapeDtypeStruct((1, width), f32),
        ),
        [smem()] + [vmem()] * 7,
        [pltpu.VMEM((tokens, width), f32)] * 4,
        dots_flops,
        12_000_000,
        (pos, rows, scale_all, all_a, all_b, eff_gate, eff_up, eff_down),
    )
    got = lax.all_to_all(both.reshape(-1, mine, 2 * width), "row", 0, 0, tiled=True)
    gain_grad = jnp.sum(from_everyone(gain_part, "row"), axis=(0, 1))
    gate_wgrad, up_wgrad, down_wgrad = call(
        weights_kernel,
        (
            jax.ShapeDtypeStruct(w_gate.shape, bf16),
            jax.ShapeDtypeStruct(w_up.shape, bf16),
            jax.ShapeDtypeStruct(w_down.shape, bf16),
        ),
        [smem()] * 4 + [vmem()] * 5,
        [pltpu.VMEM((tokens, 2 * width), bf16)] * 2,
        dots_flops,
        12_000_000,
        (pos, mask_gate, mask_up, mask_down, rows, gain, scale_all, all_a, all_b),
    )
    got = jnp.sum(up32(got), axis=0)
    x_float = up32(layer_input)
    layer_out = (x_float + got[:, :width]).astype(bf16)
    scale = lax.dynamic_slice_in_dim(scale_all, row * mine, mine, 0)
    dots = lax.dynamic_slice_in_dim(dots_all, row * mine, mine, 0)[:, None]
    input_grad = (
        up32(out_grad) + scale * gain * got[:, width:] - x_float * scale * scale * dots / D
    ).astype(bf16)
    return (layer_out, input_grad, gain_grad, gate_wgrad, up_wgrad, down_wgrad)


def solution(mesh):
    torus = Mesh(mesh.devices.reshape(mesh.shape["row"], NZ, NX), ALL)
    placed = (
        P("row", COL),
        P(COL),
        P(COL, "row"),
        P(COL, "row"),
        P("row", COL),
        P(COL, "row"),
        P(COL, "row"),
        P("row", COL),
        P("row", COL),
    )
    return jax.shard_map(
        shards,
        mesh=torus,
        in_specs=placed,
        out_specs=(
            P("row", COL),
            P("row", COL),
            P(COL),
            P(COL, "row"),
            P(COL, "row"),
            P("row", COL),
        ),
        check_vma=False,
    )
```

```python
import jax
import jax.numpy as jnp
from jax import lax
from jax.experimental import pallas as pl
from jax.experimental.pallas import tpu as pltpu
from jax.sharding import Mesh
from jax.sharding import PartitionSpec as P

D = 8192
BLK = 128
NZ, NX = 8, 4
HA, HB = 1024, 768
COL = ("col_0", "col_1")
ALL = ("row", "col_0", "col_1")
norm_eps = 1e-05

f32 = jnp.float32
bf16 = jnp.bfloat16
VMEM_BYTES = 56 * 1024 * 1024


def vmem():
    return pl.BlockSpec(memory_space=pltpu.VMEM)


def smem():
    return pl.BlockSpec(memory_space=pltpu.SMEM)


def call(kernel, outs, in_specs, scratch, flops, nbytes, args):
    return pl.pallas_call(
        kernel,
        out_shape=outs,
        in_specs=in_specs,
        out_specs=tuple(vmem() for _ in outs),
        scratch_shapes=scratch,
        compiler_params=pltpu.CompilerParams(vmem_limit_bytes=VMEM_BYTES),
        cost_estimate=pl.CostEstimate(flops=flops, bytes_accessed=nbytes, transcendentals=0),
    )(*args)


def nn(a, b):
    return jnp.dot(a, b, preferred_element_type=f32)


def nt(a, b):
    return lax.dot_general(a, b, (((1,), (1,)), ((), ())), preferred_element_type=f32)


def tn(a, b):
    return lax.dot_general(a, b, (((0,), (0,)), ((), ())), preferred_element_type=f32)


def parts3(v):
    hi = v.astype(bf16)
    rest = v - hi.astype(f32)
    mid = rest.astype(bf16)
    return hi, mid, (rest - mid.astype(f32)).astype(bf16)


def lane_sum(block, at):
    return sum(block[:, i : i + 1].astype(f32) for i in range(at, at + 3))


def pieces_of_tokens(z):
    for tz in range(NZ):
        k = lax.rem(tz - z + NZ, NZ)
        for tx in range(NX):
            nat = slice(tz * 64 + tx * 16, tz * 64 + tx * 16 + 16)
            in_a = slice((tx * NZ + tz) * 16, (tx * NZ + tz) * 16 + 16)
            in_b = pl.ds(pl.multiple_of(k * 64 + tx * 16, 16), 16)
            yield nat, in_a, in_b


def masks_kernel(mg, mu, md, wg, wu, wd, eff_g, eff_u, eff_d):
    for w, m, e in ((wg, mg, eff_g), (wu, mu, eff_u), (wd, md, eff_d)):
        for a in range(w.shape[0] // BLK):
            for b in range(w.shape[1] // BLK):
                r, c = slice(a * BLK, (a + 1) * BLK), slice(b * BLK, (b + 1) * BLK)
                e[r, c] = w[r, c] * m[a, b].astype(f32).astype(bf16)


def partials_kernel(pos, rows, gain, eff_g, eff_u, eff_d, part_a, part_b, la, lb):
    width = gain.shape[1]
    for nat, in_a, in_b in pieces_of_tokens(pos[1]):
        x = (rows[nat, :width].astype(f32) * gain[...]).astype(bf16)
        g = rows[nat, width:]
        sq = jnp.square(rows[nat, :width].astype(f32))
        part_b[in_b, 3 * HB :] = (sq[:, :BLK] + sq[:, BLK:]).astype(bf16)
        la[in_a, :width] = x
        lb[in_b, :width] = x
        la[in_a, width:] = g
        lb[in_b, width:] = g
    for left, part, at, half in ((lb, part_b, HA, HB), (la, part_a, 0, HA)):
        cols = slice(at, at + half)
        for t in range(0, left.shape[0], 128):
            tok = slice(t, t + 128)
            x, g = left[tok, :width], left[tok, width:]
            part[tok, :half] = nn(x, eff_g[:, cols]).astype(bf16)
            part[tok, half : 2 * half] = nn(x, eff_u[:, cols]).astype(bf16)
            part[tok, 2 * half : 3 * half] = nt(g, eff_d[cols, :]).astype(bf16)


def fetch_pieces(pieces, gb, sems):
    copies, at = [], 0
    for i, p in enumerate(pieces):
        copies.append(pltpu.make_async_copy(p, gb.at[pl.ds(at, p.shape[0])], sems.at[i]))
        copies[-1].start()
        at += p.shape[0]
    return copies


def features_kernel(pos, rows, ga, eff_g, eff_u, eff_d, *rest):
    pieces, (both, own_scale, gb, da, na, db, nb, sems) = rest[:-8], rest[-8:]
    copies = fetch_pieces(pieces, gb, sems)
    width = eff_g.shape[0]
    for hid, d, n, at, half in ((ga, da, na, 0, HA), (gb, db, nb, HA, HB)):
        if at:
            for c in copies:
                c.wait()
        cols = slice(at, at + half)
        for t in range(0, hid.shape[0], 128):
            tok = slice(t, t + 128)
            d[tok, :] = nn(hid[tok, :half], eff_d[cols, :])
            n[tok, :] = nt(hid[tok, half : 2 * half], eff_g[:, cols]) + nt(
                hid[tok, 2 * half : 3 * half], eff_u[:, cols]
            )
    total = jnp.zeros((16, width), f32)
    for nat, in_a, in_b in pieces_of_tokens(pos[1]):
        extra = ga[in_a, 3 * HA :]
        both[nat, :width] = (da[in_a, :] + db[in_b, :]).astype(bf16)
        grad = na[in_a, :] + nb[in_b, :]
        both[nat, width : 2 * width] = grad.astype(bf16)
        total += grad * rows[nat, :width].astype(f32) * lane_sum(extra, 0)
    gain_row = jnp.sum(total, axis=0, keepdims=True)
    lane = lax.broadcasted_iota(jnp.int32, (64, BLK), 1)
    line = lax.broadcasted_iota(jnp.int32, (64, BLK), 0)
    shared = jnp.zeros((64, BLK), f32)
    for c in range(width // 64):
        half_row = gain_row[:, (c // 2) * BLK : (c // 2 + 1) * BLK]
        picked = jnp.where(lane == line + 64 * (c % 2), half_row, 0.0)
        for i, v in enumerate(parts3(jnp.sum(picked, axis=1, keepdims=True))):
            shared = jnp.where(lane == 3 + 3 * c + i, v.astype(f32), shared)
    shared = shared.astype(bf16)
    lane16 = lax.broadcasted_iota(jnp.int32, (16, BLK), 1)
    for tz in range(NZ):
        for tx in range(NX):
            nat = slice(tz * 64 + tx * 16, tz * 64 + tx * 16 + 16)
            extra = ga[(tx * NZ + tz) * 16 : (tx * NZ + tz) * 16 + 16, 3 * HA :].astype(f32)
            moved = jnp.where(lane16 < 3, pltpu.roll(extra, BLK - 3, 1), 0.0)
            both[nat, 2 * width :] = shared[tx * 16 : tx * 16 + 16, :] + moved.astype(bf16)
    for tx in range(NX):
        at = pl.ds(pl.multiple_of(tx * 128 + pos[0] * 16, 16), 16)
        s = lane_sum(ga[at, 3 * HA :], 0)
        own_scale[tx * 16 : tx * 16 + 16, :] = jnp.broadcast_to(s, (16, BLK))


def weights_kernel(pos, mg, mu, md, rows, gain, ga, *rest):
    pieces, (out_g, out_u, out_d, gb, la, lb, sems) = rest[:-7], rest[-7:]
    copies = fetch_pieces(pieces, gb, sems)
    width = gain.shape[1]
    for nat, in_a, in_b in pieces_of_tokens(pos[1]):
        scale = lane_sum(ga[in_a, 3 * HA :], 0)
        x = (rows[nat, :width].astype(f32) * scale * gain[...]).astype(bf16)
        g = rows[nat, width:]
        la[in_a, :width] = x
        lb[in_b, :width] = x
        la[in_a, width:] = g
        lb[in_b, width:] = g
    for hid, left, at, half in ((ga, la, 0, HA), (gb, lb, HA, HB)):
        if at:
            for c in copies:
                c.wait()
        normed, grad = left[:, :width], left[:, width:]
        for c in range(0, half, BLK):
            b = (at + c) // BLK
            gw = tn(normed, hid[:, half + c : half + c + BLK])
            uw = tn(normed, hid[:, 2 * half + c : 2 * half + c + BLK])
            dw = tn(hid[:, c : c + BLK], grad)
            to = slice(at + c, at + c + BLK)
            for a in range(width // BLK):
                r = slice(a * BLK, (a + 1) * BLK)
                out_g[r, to] = (gw[r, :] * mg[a, b].astype(f32)).astype(bf16)
                out_u[r, to] = (uw[r, :] * mu[a, b].astype(f32)).astype(bf16)
                out_d[to, r] = (dw[:, r] * md[b, a].astype(f32)).astype(bf16)


def final_kernel(got, x, grad, gain, scale, layer_out, input_grad, gain_grad):
    width = gain.shape[1]
    s = got[0].astype(f32)
    for r in range(1, got.shape[0]):
        s = s + got[r].astype(f32)
    xf = x[...].astype(f32)
    layer_out[...] = (xf + s[:, :width]).astype(bf16)
    extra = s[:, 2 * width :]
    dots = lane_sum(extra, 0)
    sc = scale[:, :1]
    input_grad[...] = (
        grad[...].astype(f32)
        + sc * gain[...] * s[:, width : 2 * width]
        - xf * sc * sc * (dots / D)
    ).astype(bf16)
    lane = lax.broadcasted_iota(jnp.int32, (64, BLK), 1)
    line = lax.broadcasted_iota(jnp.int32, (64, BLK), 0)
    for h in range(width // BLK):
        spread = jnp.where(
            lane < 64,
            jnp.where(lane == line, lane_sum(extra, 3 + 6 * h), 0.0),
            jnp.where(lane == line + 64, lane_sum(extra, 6 + 6 * h), 0.0),
        )
        gain_grad[:, h * BLK : (h + 1) * BLK] = jnp.sum(spread, axis=0, keepdims=True)


def send(v, axis, step):
    n = lax.axis_size(axis)
    return lax.ppermute(v, axis, [(i, (i + step) % n) for i in range(n)])


def up32(v):
    return v.astype(f32)


def add_top(piece, got, h):
    return jnp.concatenate([(up32(piece[:h]) + up32(got)).astype(bf16), piece[h:].astype(bf16)])


def add_bottom(piece, got, h):
    return jnp.concatenate([piece[:h].astype(bf16), (up32(piece[h:]) + up32(got)).astype(bf16)])


def plus(piece, got):
    return (up32(piece) + up32(got)).astype(bf16)


def reduce_ring(pieces, axis):
    n = len(pieces)
    far = pieces[n // 2].astype(bf16)
    h = far.shape[0] // 2
    right, left = send(far[:h], axis, 1), send(far[h:], axis, -1)
    for away in range(n // 2 - 1, 0, -1):
        to_right, to_left = pieces[away], pieces[n - away]
        if away == n // 2 - 1:
            right = send(add_top(to_right, right, h), axis, 1)
            left = send(add_bottom(to_left, left, h), axis, -1)
        else:
            right = send(plus(to_right, right), axis, 1)
            left = send(plus(to_left, left), axis, -1)
    return up32(pieces[0]) + up32(right) + up32(left)


def gather_ring(shard, axis):
    n = lax.axis_size(axis)
    h = shard.shape[0] // 2
    from_right, from_left = [], []
    right = left = shard
    for _ in range(1, n // 2):
        right, left = send(right, axis, 1), send(left, axis, -1)
        from_left.insert(0, right)
        from_right.append(left)
    far = [send(right[:h], axis, 1), send(left[h:], axis, -1)]
    return [shard, *from_right, *far, *from_left]


def cut(v, n):
    m = v.shape[0] // n
    return [v[i * m : (i + 1) * m] for i in range(n)]


def hidden_grads(sums, half, scale):
    gate, up = sums[:, :half] * scale, sums[:, half : 2 * half] * scale
    act_grad = sums[:, 2 * half : 3 * half]
    sig = jax.nn.sigmoid(gate)
    act = (gate * sig * up).astype(bf16)
    gate_grad = (act_grad * up * sig * (1.0 + gate * (1.0 - sig))).astype(bf16)
    up_grad = (act_grad * gate * sig).astype(bf16)
    dots = jnp.sum(up32(gate_grad) * gate + up32(up_grad) * up, axis=1, keepdims=True)
    return [act, gate_grad, up_grad], dots


def split3(v):
    hi = lax.reduce_precision(v, 8, 7)
    mid = lax.reduce_precision(v - hi, 8, 7)
    return [hi, mid, v - hi - mid]


def exchange(v, axis):
    n = lax.axis_size(axis)
    got = lax.all_to_all(v.reshape(n, -1, v.shape[-1]), axis, 0, 0, tiled=True)
    return jnp.sum(up32(got), axis=0)


def from_everyone(shard, axis):
    copies = jnp.broadcast_to(shard, (lax.axis_size(axis), *shard.shape))
    got = lax.all_to_all(copies, axis, split_axis=0, concat_axis=0, tiled=True)
    return got.reshape(-1, shard.shape[-1])


def shape(v):
    return jax.ShapeDtypeStruct(v.shape, v.dtype)


def shards(layer_input, norm_gain, w_gate, w_up, w_down, mask_gate, mask_up, mask_down, out_grad):
    row, z = lax.axis_index("row"), lax.axis_index("col_0")
    pos = jnp.stack([row, z]).astype(jnp.int32)
    gain = norm_gain[None, :]
    mine, width = layer_input.shape
    hidden = w_gate.shape[1]
    rows = from_everyone(jnp.concatenate([layer_input, out_grad], axis=1), "row")
    tokens = rows.shape[0]
    flops = 2 * tokens * width * hidden * 3
    eff = call(
        masks_kernel,
        (shape(w_gate), shape(w_up), shape(w_down)),
        [smem()] * 3 + [vmem()] * 3,
        [],
        0,
        6_000_000,
        (mask_gate, mask_up, mask_down, w_gate, w_up, w_down),
    )
    part_a, part_b = call(
        partials_kernel,
        (
            jax.ShapeDtypeStruct((tokens, 3 * HA), bf16),
            jax.ShapeDtypeStruct((tokens, 3 * HB + BLK), bf16),
        ),
        [smem()] + [vmem()] * 5,
        [pltpu.VMEM((tokens, 2 * width), bf16)] * 2,
        flops,
        9_000_000,
        (pos, rows, gain, *eff),
    )
    sums_b = exchange(reduce_ring(cut(part_b, NZ), "col_0").astype(bf16), "col_1")
    sums_a = exchange(exchange(part_a, "col_1").astype(bf16), "col_0")
    squares = jnp.sum(sums_b[:, 3 * HB :], axis=1, keepdims=True)
    scale = lax.rsqrt(squares / D + norm_eps)
    hid_b, dots_b = hidden_grads(sums_b, HB, scale)
    hid_a, dots_a = hidden_grads(sums_a, HA, scale)
    extra = jnp.concatenate(split3(scale) + split3(dots_a + dots_b), axis=1)
    extra = jnp.pad(extra.astype(bf16), ((0, 0), (0, BLK - 6)))
    send_b = jnp.concatenate(hid_b, axis=1)
    send_a = jnp.concatenate([*hid_a, extra], axis=1)
    pieces_b = gather_ring(from_everyone(send_b, "col_1"), "col_0")
    all_a = from_everyone(from_everyone(send_a, "col_0"), "col_1")

    anywhere = [pl.BlockSpec(memory_space=pl.ANY)] * len(pieces_b)
    gb = pltpu.VMEM((tokens, 3 * HB), bf16)
    sems = pltpu.SemaphoreType.DMA((len(pieces_b),))
    both, own_scale = call(
        features_kernel,
        (
            jax.ShapeDtypeStruct((tokens, 2 * width + BLK), bf16),
            jax.ShapeDtypeStruct((mine, BLK), f32),
        ),
        [smem()] + [vmem()] * 5 + anywhere,
        [gb, *[pltpu.VMEM((tokens, width), f32)] * 4, sems],
        flops,
        9_000_000,
        (pos, rows, all_a, *eff, *pieces_b),
    )
    got = lax.all_to_all(both.reshape(-1, mine, both.shape[1]), "row", 0, 0, tiled=True)
    gate_wgrad, up_wgrad, down_wgrad = call(
        weights_kernel,
        (shape(w_gate), shape(w_up), shape(w_down)),
        [smem()] * 4 + [vmem()] * 3 + anywhere,
        [gb, *[pltpu.VMEM((tokens, 2 * width), bf16)] * 2, sems],
        flops,
        9_000_000,
        (pos, mask_gate, mask_up, mask_down, rows, gain, all_a, *pieces_b),
    )
    layer_out, input_grad, gain_grad = call(
        final_kernel,
        (shape(layer_input), shape(out_grad), shape(gain)),
        [vmem()] * 5,
        [],
        0,
        1_000_000,
        (got, layer_input, out_grad, gain, own_scale),
    )
    return (layer_out, input_grad, gain_grad[0], gate_wgrad, up_wgrad, down_wgrad)


def solution(mesh):
    torus = Mesh(mesh.devices.reshape(mesh.shape["row"], NZ, NX), ALL)
    placed = (
        P("row", COL),
        P(COL),
        P(COL, "row"),
        P(COL, "row"),
        P("row", COL),
        P(COL, "row"),
        P(COL, "row"),
        P("row", COL),
        P("row", COL),
    )
    return jax.shard_map(
        shards,
        mesh=torus,
        in_specs=placed,
        out_specs=(
            P("row", COL),
            P("row", COL),
            P(COL),
            P(COL, "row"),
            P(COL, "row"),
            P("row", COL),
        ),
        check_vma=False,
    )
```

```python
import jax
import jax.numpy as jnp
from jax import lax
from jax.experimental import pallas as pl
from jax.experimental.pallas import tpu as pltpu
from jax.sharding import Mesh
from jax.sharding import PartitionSpec as P

D = 8192
BLK = 128
NZ, NX = 8, 4
HA, HB = 768, 1024
COL = ("col_0", "col_1")
ALL = ("row", "col_0", "col_1")
norm_eps = 1e-05

f32 = jnp.float32
bf16 = jnp.bfloat16


def vmem():
    return pl.BlockSpec(memory_space=pltpu.VMEM)


def smem():
    return pl.BlockSpec(memory_space=pltpu.SMEM)


def call(kernel, outs, in_specs, scratch, flops, nbytes, args, mib=40, grid=()):
    whole = [pl.BlockSpec(o.shape, lambda *_, n=len(o.shape): (0,) * n) for o in outs]
    return pl.pallas_call(
        kernel,
        out_shape=outs,
        grid=grid,
        in_specs=in_specs,
        out_specs=tuple(whole if grid else [vmem() for _ in outs]),
        scratch_shapes=scratch,
        compiler_params=pltpu.CompilerParams(vmem_limit_bytes=mib * 1024 * 1024),
        cost_estimate=pl.CostEstimate(flops=flops, bytes_accessed=nbytes, transcendentals=0),
    )(*args)


def nn(a, b):
    return jnp.dot(a, b, preferred_element_type=f32)


def nt(a, b):
    return lax.dot_general(a, b, (((1,), (1,)), ((), ())), preferred_element_type=f32)


def tn(a, b):
    return lax.dot_general(a, b, (((0,), (0,)), ((), ())), preferred_element_type=f32)


def parts3(v):
    hi = v.astype(bf16)
    rest = v - hi.astype(f32)
    mid = rest.astype(bf16)
    return hi, mid, (rest - mid.astype(f32)).astype(bf16)


def lane_sum(block, at):
    return sum(block[:, i : i + 1].astype(f32) for i in range(at, at + 3))


def pieces_of_tokens(pos):
    for tz in range(NZ):
        k = lax.rem(tz - pos[1] + NZ, NZ)
        for tx in range(NX):
            j = lax.rem(tx - pos[2] + NX, NX)
            nat = slice(tz * 64 + tx * 16, tz * 64 + tx * 16 + 16)
            in_a = slice((tx * NZ + tz) * 16, (tx * NZ + tz) * 16 + 16)
            in_b = pl.ds(pl.multiple_of(k * 64 + j * 16, 16), 16)
            yield nat, in_a, in_b


def masks_kernel(mg, mu, md, wg, wu, wd, ag, au, ad, bg, bu, bd):
    for w, m, ea, eb, down in ((wg, mg, ag, bg, 0), (wu, mu, au, bu, 0), (wd, md, ad, bd, 1)):
        for a in range(w.shape[0] // BLK):
            for b in range(w.shape[1] // BLK):
                r, c = slice(a * BLK, (a + 1) * BLK), slice(b * BLK, (b + 1) * BLK)
                v = w[r, c] * m[a, b].astype(f32).astype(bf16)
                at = (a if down else b) * BLK
                to = slice(at % HA, at % HA + BLK) if at < HA else slice(at - HA, at - HA + BLK)
                e = ea if at < HA else eb
                if down:
                    e[to, c] = v
                else:
                    e[r, to] = v


def products(left, tok, eff, part, to, half):
    width = left.shape[1] // 2
    x, g = left[tok, :width], left[tok, width:]
    part[to, :half] = nn(x, eff[0][...]).astype(bf16)
    part[to, half : 2 * half] = nn(x, eff[1][...]).astype(bf16)
    part[to, 2 * half : 3 * half] = nt(g, eff[2][...]).astype(bf16)


def scaled(rows, nat, gain):
    width = gain.shape[1]
    return (rows[nat, :width].astype(f32) * gain[...]).astype(bf16)


def square_sums(rows, nat, width):
    sq = jnp.square(rows[nat, :width].astype(f32))
    return (sq[:, :BLK] + sq[:, BLK:]).astype(bf16)


def far_kernel(pos, rows, gain, eg, eu, ed, far_r, far_l, left):
    width = gain.shape[1]
    tz = lax.rem(pos[1] + NZ // 2, NZ)
    for j in range(NX):
        nat = pl.ds(pl.multiple_of(tz * 64 + lax.rem(pos[2] + j, NX) * 16, 16), 16)
        to = slice(j * 16, j * 16 + 16)
        left[to, :width] = scaled(rows, nat, gain)
        left[to, width:] = rows[nat, width:]
        far, at = (far_r, j * 16) if j < 2 else (far_l, j * 16 - 32)
        far[at : at + 16, 3 * HB :] = square_sums(rows, nat, width)
    x, g = left[:, :width], left[:, width:]
    for p, at in ((nn(x, eg[...]), 0), (nn(x, eu[...]), HB), (nt(g, ed[...]), 2 * HB)):
        far_r[:, at : at + HB] = p[:32].astype(bf16)
        far_l[:, at : at + HB] = p[32:].astype(bf16)


def part_a_kernel(rows, gain, eg, eu, ed, part, left):
    width = gain.shape[1]
    for tz in range(NZ):
        for tx in range(NX):
            nat = slice(tz * 64 + tx * 16, tz * 64 + tx * 16 + 16)
            to = slice((tx * NZ + tz) * 16, (tx * NZ + tz) * 16 + 16)
            left[to, :width] = scaled(rows, nat, gain)
            left[to, width:] = rows[nat, width:]
    for t in range(0, left.shape[0], 128):
        products(left, slice(t, t + 128), (eg, eu, ed), part, slice(t, t + 128), HA)


def part_b_kernel(pos, rows, gain, eg, eu, ed, part, left):
    width = gain.shape[1]
    for nat, _, to in pieces_of_tokens(pos):
        left[to, :width] = scaled(rows, nat, gain)
        left[to, width:] = rows[nat, width:]
        part[to, 3 * HB :] = square_sums(rows, nat, width)
    for t, n in ((192, 64), (320, 64), (64, 128), (384, 128), (0, 64)):
        products(left, slice(t, t + n), (eg, eu, ed), part, slice(t, t + n), HB)


def ring_first_kernel(right, left, piece_r, piece_l, out_r, out_l):
    h = right.shape[0]
    out_r[:h] = (piece_r[:h].astype(f32) + right[...].astype(f32)).astype(bf16)
    out_r[h:] = piece_r[h:]
    out_l[:h] = piece_l[:h]
    out_l[h:] = (piece_l[h:].astype(f32) + left[...].astype(f32)).astype(bf16)


def ring_kernel(right, left, piece_r, piece_l, *rest):
    out_r, out_l = rest[-2:]
    out_r[...] = (piece_r[...].astype(f32) + right[...].astype(f32)).astype(bf16)
    out_l[...] = (piece_l[...].astype(f32) + left[...].astype(f32)).astype(bf16)


def ring_last_kernel(right, left, piece, own, *others):
    for j, out in enumerate((own, *others)):
        at = slice(j * 16, j * 16 + 16)
        v = piece[at].astype(f32) + right[at].astype(f32) + left[at].astype(f32)
        out[...] = v.astype(out.dtype)


def hidden_grads(sums, half, scale, to_act, to_gate, to_up):
    dots = jnp.zeros((16, BLK), f32)
    for c in range(0, half, BLK):
        gate = sums(c) * scale
        up = sums(half + c) * scale
        act_grad = sums(2 * half + c)
        sig = jax.nn.sigmoid(gate)
        act = (gate * sig * up).astype(bf16)
        gate_grad = (act_grad * up * sig * (1.0 + gate * (1.0 - sig))).astype(bf16)
        up_grad = (act_grad * gate * sig).astype(bf16)
        to_act(c, act)
        to_gate(c, gate_grad)
        to_up(c, up_grad)
        dots += gate_grad.astype(f32) * gate + up_grad.astype(f32) * up
    return dots


def grads_b_kernel(own, j1, j2, j3, send, scale, dots):
    def sums(c):
        at = slice(c, c + BLK)
        v = own[:, at]
        for j in (j1, j2, j3):
            v = v + j[:, at].astype(f32)
        return v

    def store(at):
        def put(c, v):
            send[:, at + c : at + c + BLK] = v

        return put

    squares = jnp.sum(sums(3 * HB), axis=1, keepdims=True)
    sc = lax.rsqrt(squares / D + norm_eps)
    scale[...] = jnp.broadcast_to(sc, scale.shape)
    dots[...] = hidden_grads(sums, HB, sc, store(0), store(HB), store(2 * HB))


def grads_a_kernel(got, scale, dots_b, copies):
    def sums(c):
        return jnp.sum(got[:, :, c : c + BLK].astype(f32), axis=0)

    def store(at):
        def put(c, v):
            for n in range(NZ):
                copies[n, :, at + c : at + c + BLK] = v

        return put

    sc = scale[:, :1]
    dots = dots_b[...] + hidden_grads(sums, HA, sc, store(0), store(HA), store(2 * HA))
    lane = lax.broadcasted_iota(jnp.int32, (16, BLK), 1)
    extra = jnp.zeros((16, BLK), f32)
    for i, v in enumerate(parts3(sc) + parts3(jnp.sum(dots, axis=1, keepdims=True))):
        extra = jnp.where(lane == i, v.astype(f32), extra)
    store(3 * HA)(0, extra.astype(bf16))


def fetch_pieces(pieces, gb, sems):
    copies, at = [], 0
    for i, p in enumerate(pieces):
        copies.append(pltpu.make_async_copy(p, gb.at[pl.ds(at, p.shape[0])], sems.at[i]))
        copies[-1].start()
        at += p.shape[0]
    return copies


def features_kernel(pos, rows, ga, ag, au, ad, bg, bu, bd, *rest):
    pieces, (both, own_scale, gb, da, na, db, nb, sems) = rest[:-8], rest[-8:]
    copies = fetch_pieces(pieces, gb, sems)
    width = ag.shape[0]
    for hid, d, n, (eg, eu, ed), half in (
        (ga, da, na, (ag, au, ad), HA),
        (gb, db, nb, (bg, bu, bd), HB),
    ):
        if hid is gb:
            for c in copies:
                c.wait()
        for t in range(0, hid.shape[0], 128):
            tok = slice(t, t + 128)
            d[tok, :] = nn(hid[tok, :half], ed[...])
            n[tok, :] = nt(hid[tok, half : 2 * half], eg[...]) + nt(
                hid[tok, 2 * half : 3 * half], eu[...]
            )
    total = jnp.zeros((16, width), f32)
    for nat, in_a, in_b in pieces_of_tokens(pos):
        extra = ga[in_a, 3 * HA :]
        both[nat, :width] = (da[in_a, :] + db[in_b, :]).astype(bf16)
        grad = na[in_a, :] + nb[in_b, :]
        both[nat, width : 2 * width] = grad.astype(bf16)
        total += grad * rows[nat, :width].astype(f32) * lane_sum(extra, 0)
    gain_row = jnp.sum(total, axis=0, keepdims=True)
    lane = lax.broadcasted_iota(jnp.int32, (64, BLK), 1)
    line = lax.broadcasted_iota(jnp.int32, (64, BLK), 0)
    shared = jnp.zeros((64, BLK), f32)
    for c in range(width // 64):
        half_row = gain_row[:, (c // 2) * BLK : (c // 2 + 1) * BLK]
        picked = jnp.where(lane == line + 64 * (c % 2), half_row, 0.0)
        for i, v in enumerate(parts3(jnp.sum(picked, axis=1, keepdims=True))):
            shared = jnp.where(lane == 3 + 3 * c + i, v.astype(f32), shared)
    shared = shared.astype(bf16)
    lane16 = lax.broadcasted_iota(jnp.int32, (16, BLK), 1)
    for tz in range(NZ):
        for tx in range(NX):
            nat = slice(tz * 64 + tx * 16, tz * 64 + tx * 16 + 16)
            extra = ga[(tx * NZ + tz) * 16 : (tx * NZ + tz) * 16 + 16, 3 * HA :].astype(f32)
            moved = jnp.where(lane16 < 3, pltpu.roll(extra, BLK - 3, 1), 0.0)
            both[nat, 2 * width :] = shared[tx * 16 : tx * 16 + 16, :] + moved.astype(bf16)
    for tx in range(NX):
        at = pl.ds(pl.multiple_of(tx * 128 + pos[0] * 16, 16), 16)
        s = lane_sum(ga[at, 3 * HA :], 0)
        own_scale[tx * 16 : tx * 16 + 16, :] = jnp.broadcast_to(s, (16, BLK))


def weights_kernel(pos, mg, mu, md, rows, gain, ga, *rest):
    pieces, (out_g, out_u, out_d, gb, la, lb, sems) = rest[:-7], rest[-7:]
    copies = fetch_pieces(pieces, gb, sems)
    width = gain.shape[1]
    for nat, in_a, in_b in pieces_of_tokens(pos):
        scale = lane_sum(ga[in_a, 3 * HA :], 0)
        x = (rows[nat, :width].astype(f32) * scale * gain[...]).astype(bf16)
        g = rows[nat, width:]
        la[in_a, :width] = x
        lb[in_b, :width] = x
        la[in_a, width:] = g
        lb[in_b, width:] = g
    for hid, left, at, half in ((ga, la, 0, HA), (gb, lb, HA, HB)):
        if at:
            for c in copies:
                c.wait()
        normed, grad = left[:, :width], left[:, width:]
        for c in range(0, half, BLK):
            b = (at + c) // BLK
            gw = tn(normed, hid[:, half + c : half + c + BLK])
            uw = tn(normed, hid[:, 2 * half + c : 2 * half + c + BLK])
            dw = tn(hid[:, c : c + BLK], grad)
            to = slice(at + c, at + c + BLK)
            for a in range(width // BLK):
                r = slice(a * BLK, (a + 1) * BLK)
                out_g[r, to] = (gw[r, :] * mg[a, b].astype(f32)).astype(bf16)
                out_u[r, to] = (uw[r, :] * mu[a, b].astype(f32)).astype(bf16)
                out_d[to, r] = (dw[:, r] * md[b, a].astype(f32)).astype(bf16)


def final_kernel(got, x, grad, gain, scale, layer_out, input_grad, gain_grad):
    width = gain.shape[1]
    s = got[0].astype(f32)
    for r in range(1, got.shape[0]):
        s = s + got[r].astype(f32)
    xf = x[...].astype(f32)
    layer_out[...] = (xf + s[:, :width]).astype(bf16)
    extra = s[:, 2 * width :]
    dots = lane_sum(extra, 0)
    sc = scale[:, :1]
    input_grad[...] = (
        grad[...].astype(f32)
        + sc * gain[...] * s[:, width : 2 * width]
        - xf * sc * sc * (dots / D)
    ).astype(bf16)
    lane = lax.broadcasted_iota(jnp.int32, (64, BLK), 1)
    line = lax.broadcasted_iota(jnp.int32, (64, BLK), 0)
    for h in range(width // BLK):
        spread = jnp.where(
            lane < 64,
            jnp.where(lane == line, lane_sum(extra, 3 + 6 * h), 0.0),
            jnp.where(lane == line + 64, lane_sum(extra, 6 + 6 * h), 0.0),
        )
        gain_grad[:, h * BLK : (h + 1) * BLK] = jnp.sum(spread, axis=0, keepdims=True)


def send(v, axis, step):
    n = lax.axis_size(axis)
    return lax.ppermute(v, axis, [(i, (i + step) % n) for i in range(n)])


def ring_sum(far, part, gate_on):
    wide = part.shape[1]

    def piece(k):
        return pl.BlockSpec((64, wide), lambda i: (k, 0))

    block = jax.ShapeDtypeStruct((64, wide), bf16)
    right, left = (send(v, "col_0", s) for v, s in zip(far, (1, -1)))
    for away in range(NZ // 2 - 1, 0, -1):
        first, last = away == NZ // 2 - 1, away == 1
        got = pl.BlockSpec(right.shape, lambda i: (0, 0))
        right, left = call(
            ring_first_kernel if first else ring_kernel,
            (block, block),
            [got, got, piece(away), piece(NZ - away)]
            + ([pl.BlockSpec(memory_space=pl.ANY)] if last else []),
            [],
            0,
            2_500_000,
            (right, left, part, part) + ((gate_on,) if last else ()),
            mib=16,
            grid=(1,),
        )
        right, left = send(right, "col_0", 1), send(left, "col_0", -1)
    got = pl.BlockSpec(right.shape, lambda i: (0, 0))
    return call(
        ring_last_kernel,
        (
            jax.ShapeDtypeStruct((16, wide), f32),
            *[jax.ShapeDtypeStruct((16, wide), bf16)] * (NX - 1),
        ),
        [got, got, piece(0)],
        [],
        0,
        2_000_000,
        (right, left, part),
        mib=16,
        grid=(1,),
    )


def ring_gather(shard, axis):
    n = lax.axis_size(axis)
    h = shard.shape[0] // 2
    from_right, from_left = [], []
    right = left = shard
    for _ in range(1, n // 2):
        right, left = send(right, axis, 1), send(left, axis, -1)
        from_left.insert(0, right)
        from_right.append(left)
    far = [send(right[:h], axis, 1), send(left[h:], axis, -1)]
    return [shard, *from_right, *far, *from_left]


def from_everyone(shard, axis):
    copies = jnp.broadcast_to(shard, (lax.axis_size(axis), *shard.shape))
    got = lax.all_to_all(copies, axis, split_axis=0, concat_axis=0, tiled=True)
    return got.reshape(-1, shard.shape[-1])


def shape(v):
    return jax.ShapeDtypeStruct(v.shape, v.dtype)


def shards(layer_input, norm_gain, w_gate, w_up, w_down, mask_gate, mask_up, mask_down, out_grad):
    pos = jnp.stack([lax.axis_index(a) for a in ALL]).astype(jnp.int32)
    gain = norm_gain[None, :]
    mine, width = layer_input.shape
    rows = from_everyone(jnp.concatenate([layer_input, out_grad], axis=1), "row")
    tokens = rows.shape[0]
    flops = 2 * tokens * width * 3
    a_cols, b_cols = 3 * HA, 3 * HB + BLK

    def out(*dims, dtype=bf16):
        return jax.ShapeDtypeStruct(dims, dtype)

    eff = call(
        masks_kernel,
        (*[out(width, HA)] * 2, out(HA, width), *[out(width, HB)] * 2, out(HB, width)),
        [smem()] * 3 + [vmem()] * 3,
        [],
        0,
        6_000_000,
        (mask_gate, mask_up, mask_down, w_gate, w_up, w_down),
    )
    eff_a, eff_b = eff[:3], eff[3:]
    far = call(
        far_kernel,
        (out(32, b_cols), out(32, b_cols)),
        [smem()] + [vmem()] * 5,
        [pltpu.VMEM((64, 2 * width), bf16)],
        flops * HB // 8,
        2_000_000,
        (pos, rows, gain, *eff_b),
    )
    left = pltpu.VMEM((tokens, 2 * width), bf16)
    (part_a,) = call(
        part_a_kernel,
        (out(tokens, a_cols),),
        [vmem()] * 5,
        [left],
        flops * HA,
        4_000_000,
        (rows, gain, *eff_a),
    )
    (part_b,) = call(
        part_b_kernel,
        (out(tokens, b_cols),),
        [smem()] + [vmem()] * 5,
        [left],
        flops * HB,
        5_000_000,
        (pos, rows, gain, *eff_b),
    )
    got_a = lax.all_to_all(part_a.reshape(NX, -1, a_cols), "col_1", 0, 0, tiled=True)
    own, *others = ring_sum(far, part_b, got_a)
    got_b = [send(v, "col_1", j) for j, v in enumerate(others, 1)]
    sum_a = jnp.sum(got_a.astype(f32), axis=0).astype(bf16).reshape(NZ, -1, a_cols)
    got_a = lax.all_to_all(sum_a, "col_0", 0, 0, tiled=True)
    send_b, scale, dots_b = call(
        grads_b_kernel,
        (out(16, 3 * HB), out(16, BLK, dtype=f32), out(16, BLK, dtype=f32)),
        [vmem()] * 4,
        [],
        0,
        600_000,
        (own, *got_b),
        mib=16,
    )
    (copies_a,) = call(
        grads_a_kernel,
        (out(NZ, 16, a_cols + BLK),),
        [vmem()] * 3,
        [],
        0,
        1_500_000,
        (got_a, scale, dots_b),
        mib=16,
    )
    near = [send_b] + [send(send_b, "col_1", -j) for j in range(1, NX)]
    pieces_b = ring_gather(jnp.concatenate(near), "col_0")
    all_a = lax.all_to_all(copies_a, "col_0", 0, 0, tiled=True).reshape(-1, a_cols + BLK)
    all_a = from_everyone(all_a, "col_1")

    anywhere = [pl.BlockSpec(memory_space=pl.ANY)] * len(pieces_b)
    gb = pltpu.VMEM((tokens, 3 * HB), bf16)
    sems = pltpu.SemaphoreType.DMA((len(pieces_b),))
    both, own_scale = call(
        features_kernel,
        (out(tokens, 2 * width + BLK), out(mine, BLK, dtype=f32)),
        [smem()] + [vmem()] * 8 + anywhere,
        [gb, *[pltpu.VMEM((tokens, width), f32)] * 4, sems],
        flops * (HA + HB),
        9_000_000,
        (pos, rows, all_a, *eff_a, *eff_b, *pieces_b),
    )
    got = lax.all_to_all(both.reshape(-1, mine, both.shape[1]), "row", 0, 0, tiled=True)
    gate_wgrad, up_wgrad, down_wgrad = call(
        weights_kernel,
        (shape(w_gate), shape(w_up), shape(w_down)),
        [smem()] * 4 + [vmem()] * 3 + anywhere,
        [gb, left, left, sems],
        flops * (HA + HB),
        9_000_000,
        (pos, mask_gate, mask_up, mask_down, rows, gain, all_a, *pieces_b),
    )
    layer_out, input_grad, gain_grad = call(
        final_kernel,
        (shape(layer_input), shape(out_grad), shape(gain)),
        [vmem()] * 5,
        [],
        0,
        1_000_000,
        (got, layer_input, out_grad, gain, own_scale),
        mib=16,
    )
    return (layer_out, input_grad, gain_grad[0], gate_wgrad, up_wgrad, down_wgrad)


def solution(mesh):
    torus = Mesh(mesh.devices.reshape(mesh.shape["row"], NZ, NX), ALL)
    placed = (
        P("row", COL),
        P(COL),
        P(COL, "row"),
        P(COL, "row"),
        P("row", COL),
        P(COL, "row"),
        P(COL, "row"),
        P("row", COL),
        P("row", COL),
    )
    return jax.shard_map(
        shards,
        mesh=torus,
        in_specs=placed,
        out_specs=(
            P("row", COL),
            P("row", COL),
            P(COL),
            P(COL, "row"),
            P(COL, "row"),
            P("row", COL),
        ),
        check_vma=False,
    )
```

```python
import jax
import jax.numpy as jnp
from jax import lax
from jax.experimental import pallas as pl
from jax.experimental.pallas import tpu as pltpu
from jax.sharding import Mesh
from jax.sharding import PartitionSpec as P

D = 8192
BLK = 128
NZ, NX = 8, 4
HA, HB = 1024, 768
COL = ("col_0", "col_1")
ALL = ("row", "col_0", "col_1")
norm_eps = 1e-05

f32 = jnp.float32
bf16 = jnp.bfloat16


def vmem():
    return pl.BlockSpec(memory_space=pltpu.VMEM)


def smem():
    return pl.BlockSpec(memory_space=pltpu.SMEM)


def call(kernel, outs, in_specs, scratch, flops, nbytes, args, mib=56, grid=()):
    whole = [pl.BlockSpec(o.shape, lambda *_, n=len(o.shape): (0,) * n) for o in outs]
    return pl.pallas_call(
        kernel,
        out_shape=outs,
        grid=grid,
        in_specs=in_specs,
        out_specs=tuple(whole if grid else [vmem() for _ in outs]),
        scratch_shapes=scratch,
        compiler_params=pltpu.CompilerParams(vmem_limit_bytes=mib * 1024 * 1024),
        cost_estimate=pl.CostEstimate(flops=flops, bytes_accessed=nbytes, transcendentals=0),
    )(*args)


def nn(a, b):
    return jnp.dot(a, b, preferred_element_type=f32)


def nt(a, b):
    return lax.dot_general(a, b, (((1,), (1,)), ((), ())), preferred_element_type=f32)


def tn(a, b):
    return lax.dot_general(a, b, (((0,), (0,)), ((), ())), preferred_element_type=f32)


def parts3(v):
    hi = v.astype(bf16)
    rest = v - hi.astype(f32)
    mid = rest.astype(bf16)
    return hi, mid, (rest - mid.astype(f32)).astype(bf16)


def lane_sum(block, at):
    return sum(block[:, i : i + 1].astype(f32) for i in range(at, at + 3))


def pieces_of_tokens(pos):
    for tz in range(NZ):
        for tx in range(NX):
            j = lax.rem(tx - pos[2] + NX, NX)
            nat = slice(tz * 64 + tx * 16, tz * 64 + tx * 16 + 16)
            in_a = slice((tx * NZ + tz) * 16, (tx * NZ + tz) * 16 + 16)
            in_b = pl.ds(pl.multiple_of(tz * 64 + j * 16, 16), 16)
            yield nat, in_a, in_b


def masks_kernel(mg, mu, md, wg, wu, wd, ag, au, ad, bg, bu, bd):
    for w, m, ea, eb, down in ((wg, mg, ag, bg, 0), (wu, mu, au, bu, 0), (wd, md, ad, bd, 1)):
        for a in range(w.shape[0] // BLK):
            for b in range(w.shape[1] // BLK):
                r, c = slice(a * BLK, (a + 1) * BLK), slice(b * BLK, (b + 1) * BLK)
                v = w[r, c] * m[a, b].astype(f32).astype(bf16)
                at = (a if down else b) * BLK
                to = slice(at % HA, at % HA + BLK) if at < HA else slice(at - HA, at - HA + BLK)
                e = ea if at < HA else eb
                if down:
                    e[to, c] = v
                else:
                    e[r, to] = v


def products(left, tok, eff, part, to, half):
    width = left.shape[1] // 2
    x, g = left[tok, :width], left[tok, width:]
    part[to, :half] = nn(x, eff[0][...]).astype(bf16)
    part[to, half : 2 * half] = nn(x, eff[1][...]).astype(bf16)
    part[to, 2 * half : 3 * half] = nt(g, eff[2][...]).astype(bf16)


def scaled(rows, nat, gain):
    width = gain.shape[1]
    return (rows[nat, :width].astype(f32) * gain[...]).astype(bf16)


def square_sums(rows, nat, width):
    sq = jnp.square(rows[nat, :width].astype(f32))
    return (sq[:, :BLK] + sq[:, BLK:]).astype(bf16)


def part_a_kernel(rows, gain, eg, eu, ed, part, left):
    width = gain.shape[1]
    for tz in range(NZ):
        for tx in range(NX):
            nat = slice(tz * 64 + tx * 16, tz * 64 + tx * 16 + 16)
            to = slice((tx * NZ + tz) * 16, (tx * NZ + tz) * 16 + 16)
            left[to, :width] = scaled(rows, nat, gain)
            left[to, width:] = rows[nat, width:]
    for t in range(0, left.shape[0], 128):
        products(left, slice(t, t + 128), (eg, eu, ed), part, slice(t, t + 128), HA)


def part_b_kernel(pos, rows, gain, eg, eu, ed, part, left):
    width = gain.shape[1]
    for nat, _, to in pieces_of_tokens(pos):
        left[to, :width] = scaled(rows, nat, gain)
        left[to, width:] = rows[nat, width:]
        part[to, 3 * HB :] = square_sums(rows, nat, width)
    for t in range(0, left.shape[0], 128):
        products(left, slice(t, t + 128), (eg, eu, ed), part, slice(t, t + 128), HB)


def hidden_grads(sums, half, scale, to_act, to_gate, to_up):
    dots = jnp.zeros((16, BLK), f32)
    for c in range(0, half, BLK):
        gate = sums(c) * scale
        up = sums(half + c) * scale
        act_grad = sums(2 * half + c)
        sig = jax.nn.sigmoid(gate)
        act = (gate * sig * up).astype(bf16)
        gate_grad = (act_grad * up * sig * (1.0 + gate * (1.0 - sig))).astype(bf16)
        up_grad = (act_grad * gate * sig).astype(bf16)
        to_act(c, act)
        to_gate(c, gate_grad)
        to_up(c, up_grad)
        dots += gate_grad.astype(f32) * gate + up_grad.astype(f32) * up
    return dots


def grads_b_kernel(part, j1, j2, j3, send, scale, dots):
    def sums(c):
        at = slice(c, c + BLK)
        v = part[:16, at].astype(f32)
        for j in (j1, j2, j3):
            v = v + j[:, at].astype(f32)
        return v

    def store(at):
        def put(c, v):
            send[:, at + c : at + c + BLK] = v

        return put

    squares = jnp.sum(sums(3 * HB), axis=1, keepdims=True)
    sc = lax.rsqrt(squares / D + norm_eps)
    scale[...] = jnp.broadcast_to(sc, scale.shape)
    dots[...] = hidden_grads(sums, HB, sc, store(0), store(HB), store(2 * HB))


def grads_a_kernel(got, scale, dots_b, copies):
    def sums(c):
        return jnp.sum(got[:, :, c : c + BLK].astype(f32), axis=0)

    def store(at):
        def put(c, v):
            for n in range(NZ):
                copies[n, :, at + c : at + c + BLK] = v

        return put

    sc = scale[:, :1]
    dots = dots_b[...] + hidden_grads(sums, HA, sc, store(0), store(HA), store(2 * HA))
    lane = lax.broadcasted_iota(jnp.int32, (16, BLK), 1)
    extra = jnp.zeros((16, BLK), f32)
    for i, v in enumerate(parts3(sc) + parts3(jnp.sum(dots, axis=1, keepdims=True))):
        extra = jnp.where(lane == i, v.astype(f32), extra)
    store(3 * HA)(0, extra.astype(bf16))


def fetch(sources, targets, sems):
    copies = []
    for i, (a, b) in enumerate(zip(sources, targets)):
        copies.append(pltpu.make_async_copy(a, b, sems.at[i]))
        copies[-1].start()
    return copies


def features_kernel(pos, *rest):
    n = 9
    both, own_scale, da, na, db, nb = rest[n : n + 6]
    held, sems = rest[n + 6 : -1], rest[-1]
    copies = fetch(rest[:n], held, sems)
    gb, bg, bu, bd, ga, ag, au, ad, rows = held
    width = ag.shape[0]
    for hid, d, n, (eg, eu, ed), half, waits in (
        (gb, db, nb, (bg, bu, bd), HB, copies[:4]),
        (ga, da, na, (ag, au, ad), HA, copies[4:]),
    ):
        for c in waits:
            c.wait()
        for t in range(0, hid.shape[0], 128):
            tok = slice(t, t + 128)
            d[tok, :] = nn(hid[tok, :half], ed[...])
            n[tok, :] = nt(hid[tok, half : 2 * half], eg[...]) + nt(
                hid[tok, 2 * half : 3 * half], eu[...]
            )
    total = jnp.zeros((16, width), f32)
    for nat, in_a, in_b in pieces_of_tokens(pos):
        extra = ga[in_a, 3 * HA :]
        both[nat, :width] = (da[in_a, :] + db[in_b, :]).astype(bf16)
        grad = na[in_a, :] + nb[in_b, :]
        both[nat, width : 2 * width] = grad.astype(bf16)
        total += grad * rows[nat, :width].astype(f32) * lane_sum(extra, 0)
    gain_row = jnp.sum(total, axis=0, keepdims=True)
    lane = lax.broadcasted_iota(jnp.int32, (64, BLK), 1)
    line = lax.broadcasted_iota(jnp.int32, (64, BLK), 0)
    shared = jnp.zeros((64, BLK), f32)
    for c in range(width // 64):
        half_row = gain_row[:, (c // 2) * BLK : (c // 2 + 1) * BLK]
        picked = jnp.where(lane == line + 64 * (c % 2), half_row, 0.0)
        for i, v in enumerate(parts3(jnp.sum(picked, axis=1, keepdims=True))):
            shared = jnp.where(lane == 3 + 3 * c + i, v.astype(f32), shared)
    shared = shared.astype(bf16)
    lane16 = lax.broadcasted_iota(jnp.int32, (16, BLK), 1)
    for tz in range(NZ):
        for tx in range(NX):
            nat = slice(tz * 64 + tx * 16, tz * 64 + tx * 16 + 16)
            extra = ga[(tx * NZ + tz) * 16 : (tx * NZ + tz) * 16 + 16, 3 * HA :].astype(f32)
            moved = jnp.where(lane16 < 3, pltpu.roll(extra, BLK - 3, 1), 0.0)
            both[nat, 2 * width :] = shared[tx * 16 : tx * 16 + 16, :] + moved.astype(bf16)
    for tx in range(NX):
        at = pl.ds(pl.multiple_of(tx * 128 + pos[0] * 16, 16), 16)
        s = lane_sum(ga[at, 3 * HA :], 0)
        own_scale[tx * 16 : tx * 16 + 16, :] = jnp.broadcast_to(s, (16, BLK))


def weights_kernel(pos, mg, mu, md, gain, *rest):
    sources, (out_g, out_u, out_d, la, lb, rows, ga, gb, sems) = rest[:3], rest[3:]
    copies = fetch(sources, (rows, ga, gb), sems)
    copies[0].wait()
    copies[1].wait()
    width = gain.shape[1]
    for nat, in_a, in_b in pieces_of_tokens(pos):
        scale = lane_sum(ga[in_a, 3 * HA :], 0)
        x = (rows[nat, :width].astype(f32) * scale * gain[...]).astype(bf16)
        g = rows[nat, width:]
        la[in_a, :width] = x
        lb[in_b, :width] = x
        la[in_a, width:] = g
        lb[in_b, width:] = g
    for hid, left, at, half in ((ga, la, 0, HA), (gb, lb, HA, HB)):
        if at:
            copies[2].wait()
        normed, grad = left[:, :width], left[:, width:]
        for c in range(0, half, BLK):
            b = (at + c) // BLK
            gw = tn(normed, hid[:, half + c : half + c + BLK])
            uw = tn(normed, hid[:, 2 * half + c : 2 * half + c + BLK])
            dw = tn(hid[:, c : c + BLK], grad)
            to = slice(at + c, at + c + BLK)
            for a in range(width // BLK):
                r = slice(a * BLK, (a + 1) * BLK)
                out_g[r, to] = (gw[r, :] * mg[a, b].astype(f32)).astype(bf16)
                out_u[r, to] = (uw[r, :] * mu[a, b].astype(f32)).astype(bf16)
                out_d[to, r] = (dw[:, r] * md[b, a].astype(f32)).astype(bf16)


def final_kernel(got, x, grad, gain, scale, layer_out, input_grad, gain_grad):
    width = gain.shape[1]
    s = got[0].astype(f32)
    for r in range(1, got.shape[0]):
        s = s + got[r].astype(f32)
    xf = x[...].astype(f32)
    layer_out[...] = (xf + s[:, :width]).astype(bf16)
    extra = s[:, 2 * width :]
    dots = lane_sum(extra, 0)
    sc = scale[:, :1]
    input_grad[...] = (
        grad[...].astype(f32)
        + sc * gain[...] * s[:, width : 2 * width]
        - xf * sc * sc * (dots / D)
    ).astype(bf16)
    lane = lax.broadcasted_iota(jnp.int32, (64, BLK), 1)
    line = lax.broadcasted_iota(jnp.int32, (64, BLK), 0)
    for h in range(width // BLK):
        spread = jnp.where(
            lane < 64,
            jnp.where(lane == line, lane_sum(extra, 3 + 6 * h), 0.0),
            jnp.where(lane == line + 64, lane_sum(extra, 6 + 6 * h), 0.0),
        )
        gain_grad[:, h * BLK : (h + 1) * BLK] = jnp.sum(spread, axis=0, keepdims=True)


def send(v, axis, step):
    n = lax.axis_size(axis)
    return lax.ppermute(v, axis, [(i, (i + step) % n) for i in range(n)])


def from_everyone(shard, axis):
    copies = jnp.broadcast_to(shard, (lax.axis_size(axis), *shard.shape))
    got = lax.all_to_all(copies, axis, split_axis=0, concat_axis=0, tiled=True)
    return got.reshape(-1, shard.shape[-1])


def shape(v):
    return jax.ShapeDtypeStruct(v.shape, v.dtype)


def shards(layer_input, norm_gain, w_gate, w_up, w_down, mask_gate, mask_up, mask_down, out_grad):
    pos = jnp.stack([lax.axis_index(a) for a in ALL]).astype(jnp.int32)
    gain = norm_gain[None, :]
    mine, width = layer_input.shape
    rows = from_everyone(jnp.concatenate([layer_input, out_grad], axis=1), "row")
    tokens = rows.shape[0]
    flops = 2 * tokens * width * 3
    a_cols, b_cols = 3 * HA, 3 * HB + BLK

    def out(*dims, dtype=bf16):
        return jax.ShapeDtypeStruct(dims, dtype)

    eff = call(
        masks_kernel,
        (*[out(width, HA)] * 2, out(HA, width), *[out(width, HB)] * 2, out(HB, width)),
        [smem()] * 3 + [vmem()] * 3,
        [],
        0,
        6_000_000,
        (mask_gate, mask_up, mask_down, w_gate, w_up, w_down),
    )
    eff_a, eff_b = eff[:3], eff[3:]
    left = pltpu.VMEM((tokens, 2 * width), bf16)
    (part_a,) = call(
        part_a_kernel,
        (out(tokens, a_cols),),
        [vmem()] * 5,
        [left],
        flops * HA,
        4_000_000,
        (rows, gain, *eff_a),
    )
    (part_b,) = call(
        part_b_kernel,
        (out(tokens, b_cols),),
        [smem()] + [vmem()] * 5,
        [left],
        flops * HB,
        5_000_000,
        (pos, rows, gain, *eff_b),
    )
    got_a = lax.all_to_all(part_a.reshape(NX, -1, a_cols), "col_1", 0, 0, tiled=True)
    mine_b = lax.psum_scatter(part_b, "col_0", scatter_dimension=0, tiled=True)
    got_b = [send(mine_b[j * 16 : j * 16 + 16], "col_1", j) for j in range(1, NX)]
    sum_a = jnp.sum(got_a.astype(f32), axis=0).astype(bf16).reshape(NZ, -1, a_cols)
    got_a = lax.all_to_all(sum_a, "col_0", 0, 0, tiled=True)
    send_b, scale, dots_b = call(
        grads_b_kernel,
        (out(16, 3 * HB), out(16, BLK, dtype=f32), out(16, BLK, dtype=f32)),
        [vmem()] * 4,
        [],
        0,
        600_000,
        (mine_b, *got_b),
    )
    (copies_a,) = call(
        grads_a_kernel,
        (out(NZ, 16, a_cols + BLK),),
        [vmem()] * 3,
        [],
        0,
        1_500_000,
        (got_a, scale, dots_b),
    )
    near = [send_b] + [send(send_b, "col_1", -j) for j in range(1, NX)]
    all_b = lax.all_gather(jnp.concatenate(near), "col_0", axis=0, tiled=True)
    all_a = lax.all_to_all(copies_a, "col_0", 0, 0, tiled=True).reshape(-1, a_cols + BLK)
    all_a = from_everyone(all_a, "col_1")

    anywhere = pl.BlockSpec(memory_space=pl.ANY)
    sources = (all_b, *eff_b, all_a, *eff_a, rows)
    both, own_scale = call(
        features_kernel,
        (out(tokens, 2 * width + BLK), out(mine, BLK, dtype=f32)),
        [smem()] + [anywhere] * len(sources),
        [pltpu.VMEM((tokens, width), f32)] * 4
        + [pltpu.VMEM(v.shape, bf16) for v in sources]
        + [pltpu.SemaphoreType.DMA((len(sources),))],
        flops * (HA + HB),
        9_000_000,
        (pos, *sources),
    )
    got = lax.all_to_all(both.reshape(-1, mine, both.shape[1]), "row", 0, 0, tiled=True)
    gate_wgrad, up_wgrad, down_wgrad = call(
        weights_kernel,
        (shape(w_gate), shape(w_up), shape(w_down)),
        [smem()] * 4 + [vmem()] + [anywhere] * 3,
        [left, left]
        + [pltpu.VMEM(v.shape, bf16) for v in (rows, all_a, all_b)]
        + [pltpu.SemaphoreType.DMA((3,))],
        flops * (HA + HB),
        9_000_000,
        (pos, mask_gate, mask_up, mask_down, gain, rows, all_a, all_b),
    )
    layer_out, input_grad, gain_grad = call(
        final_kernel,
        (shape(layer_input), shape(out_grad), shape(gain)),
        [vmem()] * 5,
        [],
        0,
        1_000_000,
        (got, layer_input, out_grad, gain, own_scale),
    )
    return (layer_out, input_grad, gain_grad[0], gate_wgrad, up_wgrad, down_wgrad)


def solution(mesh):
    torus = Mesh(mesh.devices.reshape(mesh.shape["row"], NZ, NX), ALL)
    placed = (
        P("row", COL),
        P(COL),
        P(COL, "row"),
        P(COL, "row"),
        P("row", COL),
        P(COL, "row"),
        P(COL, "row"),
        P("row", COL),
        P("row", COL),
    )
    return jax.shard_map(
        shards,
        mesh=torus,
        in_specs=placed,
        out_specs=(
            P("row", COL),
            P("row", COL),
            P(COL),
            P(COL, "row"),
            P(COL, "row"),
            P("row", COL),
        ),
        check_vma=False,
    )
```

```python
import functools

import jax
import jax.numpy as jnp
from jax import lax
from jax.experimental import pallas as pl
from jax.experimental.pallas import tpu as pltpu
from jax.sharding import Mesh
from jax.sharding import PartitionSpec as P

D = 8192
BLK = 128
NZ, NX = 8, 4
HA, HB = 768, 1024
COL = ("col_0", "col_1")
ALL = ("row", "col_0", "col_1")
norm_eps = 1e-05

f32 = jnp.float32
bf16 = jnp.bfloat16


def vmem():
    return pl.BlockSpec(memory_space=pltpu.VMEM)


def smem():
    return pl.BlockSpec(memory_space=pltpu.SMEM)


def call(kernel, outs, in_specs, scratch, flops, nbytes, args, mib=56, grid=()):
    whole = [pl.BlockSpec(o.shape, lambda *_, n=len(o.shape): (0,) * n) for o in outs]
    return pl.pallas_call(
        kernel,
        out_shape=outs,
        grid=grid,
        in_specs=in_specs,
        out_specs=tuple(whole if grid else [vmem() for _ in outs]),
        scratch_shapes=scratch,
        compiler_params=pltpu.CompilerParams(vmem_limit_bytes=mib * 1024 * 1024),
        cost_estimate=pl.CostEstimate(flops=flops, bytes_accessed=nbytes, transcendentals=0),
    )(*args)


def nn(a, b):
    return jnp.dot(a, b, preferred_element_type=f32)


def nt(a, b):
    return lax.dot_general(a, b, (((1,), (1,)), ((), ())), preferred_element_type=f32)


def tn(a, b):
    return lax.dot_general(a, b, (((0,), (0,)), ((), ())), preferred_element_type=f32)


def parts3(v):
    hi = v.astype(bf16)
    rest = v - hi.astype(f32)
    mid = rest.astype(bf16)
    return hi, mid, (rest - mid.astype(f32)).astype(bf16)


def lane_sum(block, at):
    return sum(block[:, i : i + 1].astype(f32) for i in range(at, at + 3))


def pieces_of_tokens(pos):
    for tz in range(NZ):
        for tx in range(NX):
            j = lax.rem(tx - pos[2] + NX, NX)
            nat = slice(tz * 64 + tx * 16, tz * 64 + tx * 16 + 16)
            in_a = slice((tx * NZ + tz) * 16, (tx * NZ + tz) * 16 + 16)
            in_b = pl.ds(pl.multiple_of(tz * 64 + j * 16, 16), 16)
            yield nat, in_a, in_b


def masks_kernel(mg, mu, md, wg, wu, wd, ag, au, ad, bg, bu, bd):
    for w, m, ea, eb, down in ((wg, mg, ag, bg, 0), (wu, mu, au, bu, 0), (wd, md, ad, bd, 1)):
        for a in range(w.shape[0] // BLK):
            for b in range(w.shape[1] // BLK):
                r, c = slice(a * BLK, (a + 1) * BLK), slice(b * BLK, (b + 1) * BLK)
                v = w[r, c] * m[a, b].astype(f32).astype(bf16)
                at = (a if down else b) * BLK
                to = slice(at % HA, at % HA + BLK) if at < HA else slice(at - HA, at - HA + BLK)
                e = ea if at < HA else eb
                if down:
                    e[to, c] = v
                else:
                    e[r, to] = v


def products(left, tok, eff, part, to, half):
    width = left.shape[1] // 2
    x, g = left[tok, :width], left[tok, width:]
    part[to, :half] = nn(x, eff[0][...]).astype(bf16)
    part[to, half : 2 * half] = nn(x, eff[1][...]).astype(bf16)
    part[to, 2 * half : 3 * half] = nt(g, eff[2][...]).astype(bf16)


def scaled(rows, nat, gain):
    width = gain.shape[1]
    return (rows[nat, :width].astype(f32) * gain[...]).astype(bf16)


def square_sums(rows, nat, width):
    sq = jnp.square(rows[nat, :width].astype(f32))
    return (sq[:, :BLK] + sq[:, BLK:]).astype(bf16)


def part_a_kernel(rows, gain, eg, eu, ed, part, left):
    width = gain.shape[1]
    for tz in range(NZ):
        for tx in range(NX):
            nat = slice(tz * 64 + tx * 16, tz * 64 + tx * 16 + 16)
            to = slice((tx * NZ + tz) * 16, (tx * NZ + tz) * 16 + 16)
            left[to, :width] = scaled(rows, nat, gain)
            left[to, width:] = rows[nat, width:]
    for t in range(0, left.shape[0], 512):
        products(left, slice(t, t + 512), (eg, eu, ed), part, slice(t, t + 512), HA)


def part_b_kernel(pos, rows, gain, eg, eu, ed, part, left):
    width = gain.shape[1]
    for nat, _, to in pieces_of_tokens(pos):
        left[to, :width] = scaled(rows, nat, gain)
        left[to, width:] = rows[nat, width:]
        part[to, 3 * HB :] = square_sums(rows, nat, width)
    for t in range(0, left.shape[0], 512):
        products(left, slice(t, t + 512), (eg, eu, ed), part, slice(t, t + 512), HB)


def split_kernel(mine, after, *outs):
    for j, out in enumerate(outs, 1):
        out[...] = mine[j * 16 : j * 16 + 16, :]


def join_kernel(*refs):
    *pieces, _, out = refs
    for j, v in enumerate(pieces):
        out[j * 16 : j * 16 + 16, :] = v[...]


def hidden_grads(sums, half, scale, to_act, to_gate, to_up):
    dots = jnp.zeros((16, BLK), f32)
    for c in range(0, half, BLK):
        gate = sums(c) * scale
        up = sums(half + c) * scale
        act_grad = sums(2 * half + c)
        sig = jax.nn.sigmoid(gate)
        act = (gate * sig * up).astype(bf16)
        gate_grad = (act_grad * up * sig * (1.0 + gate * (1.0 - sig))).astype(bf16)
        up_grad = (act_grad * gate * sig).astype(bf16)
        to_act(c, act)
        to_gate(c, gate_grad)
        to_up(c, up_grad)
        dots += gate_grad.astype(f32) * gate + up_grad.astype(f32) * up
    return dots


def grads_b_kernel(part, j1, j2, j3, send, scale, dots):
    def sums(c):
        at = slice(c, c + BLK)
        v = part[:16, at].astype(f32)
        for j in (j1, j2, j3):
            v = v + j[:, at].astype(f32)
        return v

    def store(at):
        def put(c, v):
            send[:, at + c : at + c + BLK] = v

        return put

    squares = jnp.sum(sums(3 * HB), axis=1, keepdims=True)
    sc = lax.rsqrt(squares / D + norm_eps)
    scale[...] = jnp.broadcast_to(sc, scale.shape)
    dots[...] = hidden_grads(sums, HB, sc, store(0), store(HB), store(2 * HB))


def grads_a_kernel(got, scale, dots_b, copies):
    def sums(c):
        return jnp.sum(got[:, :, c : c + BLK].astype(f32), axis=0)

    def store(at):
        def put(c, v):
            for n in range(NZ):
                copies[n, :, at + c : at + c + BLK] = v

        return put

    sc = scale[:, :1]
    dots = dots_b[...] + hidden_grads(sums, HA, sc, store(0), store(HA), store(2 * HA))
    lane = lax.broadcasted_iota(jnp.int32, (16, BLK), 1)
    extra = jnp.zeros((16, BLK), f32)
    for i, v in enumerate(parts3(sc) + parts3(jnp.sum(dots, axis=1, keepdims=True))):
        extra = jnp.where(lane == i, v.astype(f32), extra)
    store(3 * HA)(0, extra.astype(bf16))


def fetch(sources, targets, sems):
    copies = []
    for i, (a, b) in enumerate(zip(sources, targets)):
        copies.append(pltpu.make_async_copy(a, b, sems.at[i]))
        copies[-1].start()
    return copies


def copies_kernel(x, grad, out):
    width = x.shape[1]
    for r in range(out.shape[0]):
        out[r, :, :width] = x[...]
        out[r, :, width:] = grad[...]


def features(hid, half, eg, eu, ed, down, norm):
    down[...] = nn(hid[:, :half], ed[...])
    norm[...] = nt(hid[:, half : 2 * half], eg[...]) + nt(hid[:, 2 * half : 3 * half], eu[...])


def features_a_kernel(pos, *rest):
    n = 4
    sums, scales, dots, own_scale, da, na = rest[n : n + 6]
    held, sems = rest[n + 6 : -1], rest[-1]
    for c in fetch(rest[:n], held, sems):
        c.wait()
    ga, eg, eu, ed = held
    width = eg.shape[0]
    features(ga, HA, eg, eu, ed, da, na)
    lane = lax.broadcasted_iota(jnp.int32, (16, BLK), 1)
    for nat, in_a, _ in pieces_of_tokens(pos):
        sums[nat, :width] = da[in_a, :]
        sums[nat, width:] = na[in_a, :]
        extra = ga[in_a, 3 * HA :].astype(f32)
        scales[nat, :] = jnp.broadcast_to(lane_sum(extra, 0), (16, BLK))
        dots[nat, :] = jnp.where(lane < 3, pltpu.roll(extra, BLK - 3, 1), 0.0).astype(bf16)
    for tx in range(NX):
        at = pl.ds(pl.multiple_of(tx * 128 + pos[0] * 16, 16), 16)
        s = lane_sum(ga[at, 3 * HA :], 0)
        own_scale[tx * 16 : tx * 16 + 16, :] = jnp.broadcast_to(s, (16, BLK))


def features_b_kernel(pos, *rest):
    n = 8
    both, db, nb = rest[n : n + 3]
    held, sems = rest[n + 3 : -1], rest[-1]
    for c in fetch(rest[:n], held, sems):
        c.wait()
    gb, eg, eu, ed, sums, scales, dots, rows = held
    width = eg.shape[0]
    features(gb, HB, eg, eu, ed, db, nb)
    total = jnp.zeros((16, width), f32)
    for nat, _, in_b in pieces_of_tokens(pos):
        both[nat, :width] = (sums[nat, :width] + db[in_b, :]).astype(bf16)
        grad = sums[nat, width:] + nb[in_b, :]
        both[nat, width : 2 * width] = grad.astype(bf16)
        total += grad * rows[nat, :width].astype(f32) * scales[nat, :1]
    gain_row = jnp.sum(total, axis=0, keepdims=True)
    lane = lax.broadcasted_iota(jnp.int32, (64, BLK), 1)
    line = lax.broadcasted_iota(jnp.int32, (64, BLK), 0)
    shared = jnp.zeros((64, BLK), f32)
    for c in range(width // 64):
        half_row = gain_row[:, (c // 2) * BLK : (c // 2 + 1) * BLK]
        picked = jnp.where(lane == line + 64 * (c % 2), half_row, 0.0)
        for i, v in enumerate(parts3(jnp.sum(picked, axis=1, keepdims=True))):
            shared = jnp.where(lane == 3 + 3 * c + i, v.astype(f32), shared)
    shared = shared.astype(bf16)
    for tz in range(NZ):
        nat = slice(tz * 64, tz * 64 + 64)
        both[nat, 2 * width :] = shared + dots[nat, :]


def weights_kernel(pos, mg, mu, md, gain, *rest):
    sources, (out_g, out_u, out_d, la, lb, rows, ga, gb, sems) = rest[:3], rest[3:]
    copies = fetch(sources, (rows, ga, gb), sems)
    copies[0].wait()
    copies[1].wait()
    width = gain.shape[1]
    for nat, in_a, in_b in pieces_of_tokens(pos):
        scale = lane_sum(ga[in_a, 3 * HA :], 0)
        x = (rows[nat, :width].astype(f32) * scale * gain[...]).astype(bf16)
        g = rows[nat, width:]
        la[in_a, :width] = x
        lb[in_b, :width] = x
        la[in_a, width:] = g
        lb[in_b, width:] = g
    for hid, left, at, half in ((ga, la, 0, HA), (gb, lb, HA, HB)):
        if at:
            copies[2].wait()
        normed, grad = left[:, :width], left[:, width:]
        for c in range(0, half, BLK):
            b = (at + c) // BLK
            gw = tn(normed, hid[:, half + c : half + c + BLK])
            uw = tn(normed, hid[:, 2 * half + c : 2 * half + c + BLK])
            dw = tn(hid[:, c : c + BLK], grad)
            to = slice(at + c, at + c + BLK)
            for a in range(width // BLK):
                r = slice(a * BLK, (a + 1) * BLK)
                out_g[r, to] = (gw[r, :] * mg[a, b].astype(f32)).astype(bf16)
                out_u[r, to] = (uw[r, :] * mu[a, b].astype(f32)).astype(bf16)
                out_d[to, r] = (dw[:, r] * md[b, a].astype(f32)).astype(bf16)


def final_kernel(got, x, grad, gain, scale, layer_out, input_grad, gain_grad):
    width = gain.shape[1]
    s = got[0].astype(f32)
    for r in range(1, got.shape[0]):
        s = s + got[r].astype(f32)
    xf = x[...].astype(f32)
    layer_out[...] = (xf + s[:, :width]).astype(bf16)
    extra = s[:, 2 * width :]
    dots = lane_sum(extra, 0)
    sc = scale[:, :1]
    input_grad[...] = (
        grad[...].astype(f32)
        + sc * gain[...] * s[:, width : 2 * width]
        - xf * sc * sc * (dots / D)
    ).astype(bf16)
    lane = lax.broadcasted_iota(jnp.int32, (64, BLK), 1)
    line = lax.broadcasted_iota(jnp.int32, (64, BLK), 0)
    for h in range(width // BLK):
        spread = jnp.where(
            lane < 64,
            jnp.where(lane == line, lane_sum(extra, 3 + 6 * h), 0.0),
            jnp.where(lane == line + 64, lane_sum(extra, 6 + 6 * h), 0.0),
        )
        gain_grad[:, h * BLK : (h + 1) * BLK] = jnp.sum(spread, axis=0, keepdims=True)


def send(v, axis, step):
    n = lax.axis_size(axis)
    return lax.ppermute(v, axis, [(i, (i + step) % n) for i in range(n)])


def from_everyone(shard, axis):
    copies = jnp.broadcast_to(shard, (lax.axis_size(axis), *shard.shape))
    got = lax.all_to_all(copies, axis, split_axis=0, concat_axis=0, tiled=True)
    return got.reshape(-1, shard.shape[-1])


def shape(v):
    return jax.ShapeDtypeStruct(v.shape, v.dtype)


def shards(layer_input, norm_gain, w_gate, w_up, w_down, mask_gate, mask_up, mask_down, out_grad):
    pos = jnp.stack([lax.axis_index(a) for a in ALL]).astype(jnp.int32)
    gain = norm_gain[None, :]
    mine, width = layer_input.shape
    n_rows = lax.axis_size("row")
    tokens = n_rows * mine
    flops = 2 * tokens * width * 3
    a_cols, b_cols = 3 * HA, 3 * HB + BLK

    def out(*dims, dtype=bf16):
        return jax.ShapeDtypeStruct(dims, dtype)

    (first,) = call(
        copies_kernel,
        (out(n_rows, mine, 2 * width),),
        [vmem()] * 2,
        [],
        0,
        600_000,
        (layer_input, out_grad),
        mib=16,
    )
    rows = lax.all_to_all(first, "row", 0, 0, tiled=True).reshape(tokens, -1)
    eff = call(
        masks_kernel,
        (*[out(width, HA)] * 2, out(HA, width), *[out(width, HB)] * 2, out(HB, width)),
        [smem()] * 3 + [vmem()] * 3,
        [],
        0,
        6_000_000,
        (mask_gate, mask_up, mask_down, w_gate, w_up, w_down),
        mib=56,
    )
    eff_a, eff_b = eff[:3], eff[3:]
    left = pltpu.VMEM((tokens, 2 * width), bf16)
    (part_a,) = call(
        part_a_kernel,
        (out(tokens, a_cols),),
        [vmem()] * 5,
        [left],
        flops * HA,
        4_000_000,
        (rows, gain, *eff_a),
        mib=56,
    )
    (part_b,) = call(
        part_b_kernel,
        (out(tokens, b_cols),),
        [smem()] + [vmem()] * 5,
        [left],
        flops * HB,
        5_000_000,
        (pos, rows, gain, *eff_b),
        mib=56,
    )
    got_a = lax.all_to_all(part_a.reshape(NX, -1, a_cols), "col_1", 0, 0, tiled=True)
    mine_b = lax.psum_scatter(part_b, "col_0", scatter_dimension=0, tiled=True)
    sum_a = jnp.sum(got_a.astype(f32), axis=0).astype(bf16).reshape(NZ, -1, a_cols)
    others = call(
        split_kernel,
        tuple([out(16, b_cols)] * (NX - 1)),
        [vmem(), pl.BlockSpec(memory_space=pl.ANY)],
        [],
        0,
        600_000,
        (mine_b, sum_a),
        mib=16,
    )
    got_b = [send(v, "col_1", j) for j, v in enumerate(others, 1)]
    got_a = lax.all_to_all(sum_a, "col_0", 0, 0, tiled=True)
    send_b, scale, dots_b = call(
        grads_b_kernel,
        (out(16, 3 * HB), out(16, BLK, dtype=f32), out(16, BLK, dtype=f32)),
        [vmem()] * 4,
        [],
        0,
        600_000,
        (mine_b, *got_b),
        mib=16,
    )
    (copies_a,) = call(
        grads_a_kernel,
        (out(NZ, 16, a_cols + BLK),),
        [vmem()] * 3,
        [],
        0,
        1_500_000,
        (got_a, scale, dots_b),
        mib=16,
    )
    near = [send_b] + [send(send_b, "col_1", -j) for j in range(1, NX)]
    (near,) = call(
        join_kernel,
        (out(NX * 16, 3 * HB),),
        [vmem()] * NX + [pl.BlockSpec(memory_space=pl.ANY)],
        [],
        0,
        600_000,
        (*near, got_a),
        mib=16,
    )
    all_b = lax.all_gather(near, "col_0", axis=0, tiled=True)
    all_a = lax.all_to_all(copies_a, "col_0", 0, 0, tiled=True).reshape(-1, a_cols + BLK)
    all_a = from_everyone(all_a, "col_1")

    anywhere = pl.BlockSpec(memory_space=pl.ANY)
    f_shape = functools.partial(out, dtype=f32)
    sources = (all_a, *eff_a)
    sums, scales, dots, own_scale = call(
        features_a_kernel,
        (f_shape(tokens, 2 * width), f_shape(tokens, BLK), out(tokens, BLK), f_shape(mine, BLK)),
        [smem()] + [anywhere] * len(sources),
        [pltpu.VMEM((tokens, width), f32)] * 2
        + [pltpu.VMEM(v.shape, v.dtype) for v in sources]
        + [pltpu.SemaphoreType.DMA((len(sources),))],
        flops * HA,
        6_000_000,
        (pos, *sources),
    )
    sources = (all_b, *eff_b, sums, scales, dots, rows)
    (both,) = call(
        features_b_kernel,
        (out(tokens, 2 * width + BLK),),
        [smem()] + [anywhere] * len(sources),
        [pltpu.VMEM((tokens, width), f32)] * 2
        + [pltpu.VMEM(v.shape, v.dtype) for v in sources]
        + [pltpu.SemaphoreType.DMA((len(sources),))],
        flops * HB,
        8_000_000,
        (pos, *sources),
    )
    got = lax.all_to_all(both.reshape(-1, mine, both.shape[1]), "row", 0, 0, tiled=True)
    gate_wgrad, up_wgrad, down_wgrad = call(
        weights_kernel,
        (shape(w_gate), shape(w_up), shape(w_down)),
        [smem()] * 4 + [vmem()] + [anywhere] * 3,
        [left, left]
        + [pltpu.VMEM(v.shape, bf16) for v in (rows, all_a, all_b)]
        + [pltpu.SemaphoreType.DMA((3,))],
        flops * (HA + HB),
        9_000_000,
        (pos, mask_gate, mask_up, mask_down, gain, rows, all_a, all_b),
    )
    layer_out, input_grad, gain_grad = call(
        final_kernel,
        (shape(layer_input), shape(out_grad), shape(gain)),
        [vmem()] * 5,
        [],
        0,
        1_000_000,
        (got, layer_input, out_grad, gain, own_scale),
        mib=16,
    )
    return (layer_out, input_grad, gain_grad[0], gate_wgrad, up_wgrad, down_wgrad)


def solution(mesh):
    torus = Mesh(mesh.devices.reshape(mesh.shape["row"], NZ, NX), ALL)
    placed = (
        P("row", COL),
        P(COL),
        P(COL, "row"),
        P(COL, "row"),
        P("row", COL),
        P(COL, "row"),
        P(COL, "row"),
        P("row", COL),
        P("row", COL),
    )
    return jax.shard_map(
        shards,
        mesh=torus,
        in_specs=placed,
        out_specs=(
            P("row", COL),
            P("row", COL),
            P(COL),
            P(COL, "row"),
            P(COL, "row"),
            P("row", COL),
        ),
        check_vma=False,
    )
```

```python
import functools

import jax
import jax.numpy as jnp
from jax import lax
from jax.experimental import pallas as pl
from jax.experimental.pallas import tpu as pltpu
from jax.sharding import Mesh
from jax.sharding import PartitionSpec as P

D = 8192
BLK = 128
NZ, NX = 8, 4
HA, HB = 768, 1024
COL = ("col_0", "col_1")
ALL = ("row", "col_0", "col_1")
norm_eps = 1e-05

f32 = jnp.float32
bf16 = jnp.bfloat16


def vmem():
    return pl.BlockSpec(memory_space=pltpu.VMEM)


def smem():
    return pl.BlockSpec(memory_space=pltpu.SMEM)


def call(kernel, outs, in_specs, scratch, flops, nbytes, args, mib=56, grid=()):
    whole = [pl.BlockSpec(o.shape, lambda *_, n=len(o.shape): (0,) * n) for o in outs]
    return pl.pallas_call(
        kernel,
        out_shape=outs,
        grid=grid,
        in_specs=in_specs,
        out_specs=tuple(whole if grid else [vmem() for _ in outs]),
        scratch_shapes=scratch,
        compiler_params=pltpu.CompilerParams(vmem_limit_bytes=mib * 1024 * 1024),
        cost_estimate=pl.CostEstimate(flops=flops, bytes_accessed=nbytes, transcendentals=0),
    )(*args)


def nn(a, b):
    return jnp.dot(a, b, preferred_element_type=f32)


def nt(a, b):
    return lax.dot_general(a, b, (((1,), (1,)), ((), ())), preferred_element_type=f32)


def tn(a, b):
    return lax.dot_general(a, b, (((0,), (0,)), ((), ())), preferred_element_type=f32)


def parts3(v):
    hi = v.astype(bf16)
    rest = v - hi.astype(f32)
    mid = rest.astype(bf16)
    return hi, mid, (rest - mid.astype(f32)).astype(bf16)


def lane_sum(block, at):
    return sum(block[:, i : i + 1].astype(f32) for i in range(at, at + 3))


def pieces_of_tokens(pos):
    for tz in range(NZ):
        for tx in range(NX):
            j = lax.rem(tx - pos[2] + NX, NX)
            nat = slice(tz * 64 + tx * 16, tz * 64 + tx * 16 + 16)
            in_a = slice((tx * NZ + tz) * 16, (tx * NZ + tz) * 16 + 16)
            in_b = pl.ds(pl.multiple_of(tz * 64 + j * 16, 16), 16)
            yield nat, in_a, in_b


def masks_kernel(mg, mu, md, wg, wu, wd, ag, au, ad, bg, bu, bd):
    for w, m, ea, eb, down in ((wg, mg, ag, bg, 0), (wu, mu, au, bu, 0), (wd, md, ad, bd, 1)):
        for a in range(w.shape[0] // BLK):
            for b in range(w.shape[1] // BLK):
                r, c = slice(a * BLK, (a + 1) * BLK), slice(b * BLK, (b + 1) * BLK)
                v = w[r, c] * m[a, b].astype(f32).astype(bf16)
                at = (a if down else b) * BLK
                to = slice(at % HA, at % HA + BLK) if at < HA else slice(at - HA, at - HA + BLK)
                e = ea if at < HA else eb
                if down:
                    e[to, c] = v
                else:
                    e[r, to] = v


def products(left, tok, eff, part, to, half):
    width = left.shape[1] // 2
    x, g = left[tok, :width], left[tok, width:]
    part[to, :half] = nn(x, eff[0][...]).astype(bf16)
    part[to, half : 2 * half] = nn(x, eff[1][...]).astype(bf16)
    part[to, 2 * half : 3 * half] = nt(g, eff[2][...]).astype(bf16)


def scaled(rows, nat, gain):
    width = gain.shape[1]
    return (rows[nat, :width].astype(f32) * gain[...]).astype(bf16)


def square_sums(rows, nat, width):
    sq = jnp.square(rows[nat, :width].astype(f32))
    return (sq[:, :BLK] + sq[:, BLK:]).astype(bf16)


def part_a_kernel(rows, gain, eg, eu, ed, part, left):
    width = gain.shape[1]
    for tz in range(NZ):
        for tx in range(NX):
            nat = slice(tz * 64 + tx * 16, tz * 64 + tx * 16 + 16)
            to = slice((tx * NZ + tz) * 16, (tx * NZ + tz) * 16 + 16)
            left[to, :width] = scaled(rows, nat, gain)
            left[to, width:] = rows[nat, width:]
    for t in range(0, left.shape[0], 512):
        products(left, slice(t, t + 512), (eg, eu, ed), part, slice(t, t + 512), HA)


def part_b_kernel(pos, rows, gain, eg, eu, ed, part, left):
    width = gain.shape[1]
    for nat, _, to in pieces_of_tokens(pos):
        left[to, :width] = scaled(rows, nat, gain)
        left[to, width:] = rows[nat, width:]
        part[to, 3 * HB :] = square_sums(rows, nat, width)
    for t in range(0, left.shape[0], 512):
        products(left, slice(t, t + 512), (eg, eu, ed), part, slice(t, t + 512), HB)


def split_kernel(mine, after, *outs):
    for j, out in enumerate(outs, 1):
        out[...] = mine[j * 16 : j * 16 + 16, :]


def join_kernel(*refs):
    *pieces, _, out = refs
    for j, v in enumerate(pieces):
        out[j * 16 : j * 16 + 16, :] = v[...]


def hidden_grads(sums, half, scale, to_act, to_gate, to_up):
    dots = jnp.zeros((16, BLK), f32)
    for c in range(0, half, BLK):
        gate = sums(c) * scale
        up = sums(half + c) * scale
        act_grad = sums(2 * half + c)
        sig = jax.nn.sigmoid(gate)
        act = (gate * sig * up).astype(bf16)
        gate_grad = (act_grad * up * sig * (1.0 + gate * (1.0 - sig))).astype(bf16)
        up_grad = (act_grad * gate * sig).astype(bf16)
        to_act(c, act)
        to_gate(c, gate_grad)
        to_up(c, up_grad)
        dots += gate_grad.astype(f32) * gate + up_grad.astype(f32) * up
    return dots


def grads_b_kernel(part, j1, j2, j3, send, scale, dots):
    def sums(c):
        at = slice(c, c + BLK)
        v = part[:16, at].astype(f32)
        for j in (j1, j2, j3):
            v = v + j[:, at].astype(f32)
        return v

    def store(at):
        def put(c, v):
            send[:, at + c : at + c + BLK] = v

        return put

    squares = jnp.sum(sums(3 * HB), axis=1, keepdims=True)
    sc = lax.rsqrt(squares / D + norm_eps)
    scale[...] = jnp.broadcast_to(sc, scale.shape)
    dots[...] = hidden_grads(sums, HB, sc, store(0), store(HB), store(2 * HB))


def grads_a_kernel(got, scale, dots_b, copies):
    def sums(c):
        return jnp.sum(got[:, :, c : c + BLK].astype(f32), axis=0)

    def store(at):
        def put(c, v):
            for n in range(NZ):
                copies[n, :, at + c : at + c + BLK] = v

        return put

    sc = scale[:, :1]
    dots = dots_b[...] + hidden_grads(sums, HA, sc, store(0), store(HA), store(2 * HA))
    lane = lax.broadcasted_iota(jnp.int32, (16, BLK), 1)
    extra = jnp.zeros((16, BLK), f32)
    for i, v in enumerate(parts3(sc) + parts3(jnp.sum(dots, axis=1, keepdims=True))):
        extra = jnp.where(lane == i, v.astype(f32), extra)
    store(3 * HA)(0, extra.astype(bf16))


def fetch(sources, targets, sems):
    copies = []
    for i, (a, b) in enumerate(zip(sources, targets)):
        copies.append(pltpu.make_async_copy(a, b, sems.at[i]))
        copies[-1].start()
    return copies


def copies_kernel(x, grad, out):
    width = x.shape[1]
    for r in range(out.shape[0]):
        out[r, :, :width] = x[...]
        out[r, :, width:] = grad[...]


def features(hid, half, eg, eu, ed, down, norm):
    down[...] = nn(hid[:, :half], ed[...])
    norm[...] = nt(hid[:, half : 2 * half], eg[...]) + nt(hid[:, 2 * half : 3 * half], eu[...])


def features_a_kernel(pos, *rest):
    n = 4
    sums, scales, dots, own_scale, da, na = rest[n : n + 6]
    held, sems = rest[n + 6 : -1], rest[-1]
    for c in fetch(rest[:n], held, sems):
        c.wait()
    ga, eg, eu, ed = held
    width = eg.shape[0]
    features(ga, HA, eg, eu, ed, da, na)
    lane = lax.broadcasted_iota(jnp.int32, (16, BLK), 1)
    for nat, in_a, _ in pieces_of_tokens(pos):
        sums[nat, :width] = da[in_a, :]
        sums[nat, width:] = na[in_a, :]
        extra = ga[in_a, 3 * HA :].astype(f32)
        scales[nat, :] = jnp.broadcast_to(lane_sum(extra, 0), (16, BLK))
        dots[nat, :] = jnp.where(lane < 3, pltpu.roll(extra, BLK - 3, 1), 0.0).astype(bf16)
    for tx in range(NX):
        at = pl.ds(pl.multiple_of(tx * 128 + pos[0] * 16, 16), 16)
        s = lane_sum(ga[at, 3 * HA :], 0)
        own_scale[tx * 16 : tx * 16 + 16, :] = jnp.broadcast_to(s, (16, BLK))


def features_b_kernel(pos, *rest):
    n = 8
    both, db, nb = rest[n : n + 3]
    held, sems = rest[n + 3 : -1], rest[-1]
    copies = fetch(rest[:n], held, sems)
    for c in copies[:4]:
        c.wait()
    gb, eg, eu, ed, sums, scales, dots, rows = held
    width = eg.shape[0]
    features(gb, HB, eg, eu, ed, db, nb)
    for c in copies[4:]:
        c.wait()
    total = jnp.zeros((16, width), f32)
    for nat, _, in_b in pieces_of_tokens(pos):
        both[nat, :width] = (sums[nat, :width] + db[in_b, :]).astype(bf16)
        grad = sums[nat, width:] + nb[in_b, :]
        both[nat, width : 2 * width] = grad.astype(bf16)
        total += grad * rows[nat, :width].astype(f32) * scales[nat, :1]
    gain_row = jnp.sum(total, axis=0, keepdims=True)
    lane = lax.broadcasted_iota(jnp.int32, (64, BLK), 1)
    line = lax.broadcasted_iota(jnp.int32, (64, BLK), 0)
    shared = jnp.zeros((64, BLK), f32)
    for c in range(width // 64):
        half_row = gain_row[:, (c // 2) * BLK : (c // 2 + 1) * BLK]
        picked = jnp.where(lane == line + 64 * (c % 2), half_row, 0.0)
        for i, v in enumerate(parts3(jnp.sum(picked, axis=1, keepdims=True))):
            shared = jnp.where(lane == 3 + 3 * c + i, v.astype(f32), shared)
    shared = shared.astype(bf16)
    for tz in range(NZ):
        nat = slice(tz * 64, tz * 64 + 64)
        both[nat, 2 * width :] = shared + dots[nat, :]


def weights_kernel(pos, mg, mu, md, gain, *rest):
    sources, (out_g, out_u, out_d, la, lb, rows, ga, gb, sems) = rest[:3], rest[3:]
    copies = fetch(sources, (rows, ga, gb), sems)
    copies[0].wait()
    copies[1].wait()
    width = gain.shape[1]
    for nat, in_a, in_b in pieces_of_tokens(pos):
        scale = lane_sum(ga[in_a, 3 * HA :], 0)
        x = (rows[nat, :width].astype(f32) * scale * gain[...]).astype(bf16)
        g = rows[nat, width:]
        la[in_a, :width] = x
        lb[in_b, :width] = x
        la[in_a, width:] = g
        lb[in_b, width:] = g
    for hid, left, at, half in ((ga, la, 0, HA), (gb, lb, HA, HB)):
        if at:
            copies[2].wait()
        normed, grad = left[:, :width], left[:, width:]
        for c in range(0, half, BLK):
            b = (at + c) // BLK
            gw = tn(normed, hid[:, half + c : half + c + BLK])
            uw = tn(normed, hid[:, 2 * half + c : 2 * half + c + BLK])
            dw = tn(hid[:, c : c + BLK], grad)
            to = slice(at + c, at + c + BLK)
            for a in range(width // BLK):
                r = slice(a * BLK, (a + 1) * BLK)
                out_g[r, to] = (gw[r, :] * mg[a, b].astype(f32)).astype(bf16)
                out_u[r, to] = (uw[r, :] * mu[a, b].astype(f32)).astype(bf16)
                out_d[to, r] = (dw[:, r] * md[b, a].astype(f32)).astype(bf16)


def final_kernel(got, x, grad, gain, scale, layer_out, input_grad, gain_grad):
    width = gain.shape[1]
    s = got[0].astype(f32)
    for r in range(1, got.shape[0]):
        s = s + got[r].astype(f32)
    xf = x[...].astype(f32)
    layer_out[...] = (xf + s[:, :width]).astype(bf16)
    extra = s[:, 2 * width :]
    dots = lane_sum(extra, 0)
    sc = scale[:, :1]
    input_grad[...] = (
        grad[...].astype(f32)
        + sc * gain[...] * s[:, width : 2 * width]
        - xf * sc * sc * (dots / D)
    ).astype(bf16)
    lane = lax.broadcasted_iota(jnp.int32, (64, BLK), 1)
    line = lax.broadcasted_iota(jnp.int32, (64, BLK), 0)
    for h in range(width // BLK):
        spread = jnp.where(
            lane < 64,
            jnp.where(lane == line, lane_sum(extra, 3 + 6 * h), 0.0),
            jnp.where(lane == line + 64, lane_sum(extra, 6 + 6 * h), 0.0),
        )
        gain_grad[:, h * BLK : (h + 1) * BLK] = jnp.sum(spread, axis=0, keepdims=True)


def send(v, axis, step):
    n = lax.axis_size(axis)
    return lax.ppermute(v, axis, [(i, (i + step) % n) for i in range(n)])


def from_everyone(shard, axis):
    copies = jnp.broadcast_to(shard, (lax.axis_size(axis), *shard.shape))
    got = lax.all_to_all(copies, axis, split_axis=0, concat_axis=0, tiled=True)
    return got.reshape(-1, shard.shape[-1])


def shape(v):
    return jax.ShapeDtypeStruct(v.shape, v.dtype)


def shards(layer_input, norm_gain, w_gate, w_up, w_down, mask_gate, mask_up, mask_down, out_grad):
    pos = jnp.stack([lax.axis_index(a) for a in ALL]).astype(jnp.int32)
    gain = norm_gain[None, :]
    mine, width = layer_input.shape
    n_rows = lax.axis_size("row")
    tokens = n_rows * mine
    flops = 2 * tokens * width * 3
    a_cols, b_cols = 3 * HA, 3 * HB + BLK

    def out(*dims, dtype=bf16):
        return jax.ShapeDtypeStruct(dims, dtype)

    (first,) = call(
        copies_kernel,
        (out(n_rows, mine, 2 * width),),
        [vmem()] * 2,
        [],
        0,
        600_000,
        (layer_input, out_grad),
        mib=56,
    )
    rows = lax.all_to_all(first, "row", 0, 0, tiled=True).reshape(tokens, -1)
    eff = call(
        masks_kernel,
        (*[out(width, HA)] * 2, out(HA, width), *[out(width, HB)] * 2, out(HB, width)),
        [smem()] * 3 + [vmem()] * 3,
        [],
        0,
        6_000_000,
        (mask_gate, mask_up, mask_down, w_gate, w_up, w_down),
        mib=56,
    )
    eff_a, eff_b = eff[:3], eff[3:]
    left = pltpu.VMEM((tokens, 2 * width), bf16)
    (part_a,) = call(
        part_a_kernel,
        (out(tokens, a_cols),),
        [vmem()] * 5,
        [left],
        flops * HA,
        4_000_000,
        (rows, gain, *eff_a),
        mib=56,
    )
    (part_b,) = call(
        part_b_kernel,
        (out(tokens, b_cols),),
        [smem()] + [vmem()] * 5,
        [left],
        flops * HB,
        5_000_000,
        (pos, rows, gain, *eff_b),
        mib=56,
    )
    got_a = lax.all_to_all(part_a.reshape(NX, -1, a_cols), "col_1", 0, 0, tiled=True)
    mine_b = lax.psum_scatter(part_b, "col_0", scatter_dimension=0, tiled=True)
    sum_a = jnp.sum(got_a.astype(f32), axis=0).astype(bf16).reshape(NZ, -1, a_cols)
    others = call(
        split_kernel,
        tuple([out(16, b_cols)] * (NX - 1)),
        [vmem(), pl.BlockSpec(memory_space=pl.ANY)],
        [],
        0,
        600_000,
        (mine_b, sum_a),
        mib=16,
    )
    got_b = [send(v, "col_1", j) for j, v in enumerate(others, 1)]
    got_a = lax.all_to_all(sum_a, "col_0", 0, 0, tiled=True)
    send_b, scale, dots_b = call(
        grads_b_kernel,
        (out(16, 3 * HB), out(16, BLK, dtype=f32), out(16, BLK, dtype=f32)),
        [vmem()] * 4,
        [],
        0,
        600_000,
        (mine_b, *got_b),
        mib=16,
    )
    (copies_a,) = call(
        grads_a_kernel,
        (out(NZ, 16, a_cols + BLK),),
        [vmem()] * 3,
        [],
        0,
        1_500_000,
        (got_a, scale, dots_b),
        mib=16,
    )
    near = [send_b] + [send(send_b, "col_1", -j) for j in range(1, NX)]
    (near,) = call(
        join_kernel,
        (out(NX * 16, 3 * HB),),
        [vmem()] * NX + [pl.BlockSpec(memory_space=pl.ANY)],
        [],
        0,
        600_000,
        (*near, got_a),
        mib=16,
    )
    all_b = lax.all_gather(near, "col_0", axis=0, tiled=True)
    all_a = lax.all_to_all(copies_a, "col_0", 0, 0, tiled=True).reshape(-1, a_cols + BLK)
    all_a = from_everyone(all_a, "col_1")

    anywhere = pl.BlockSpec(memory_space=pl.ANY)
    f_shape = functools.partial(out, dtype=f32)
    sources = (all_a, *eff_a)
    sums, scales, dots, own_scale = call(
        features_a_kernel,
        (f_shape(tokens, 2 * width), f_shape(tokens, BLK), out(tokens, BLK), f_shape(mine, BLK)),
        [smem()] + [anywhere] * len(sources),
        [pltpu.VMEM((tokens, width), f32)] * 2
        + [pltpu.VMEM(v.shape, v.dtype) for v in sources]
        + [pltpu.SemaphoreType.DMA((len(sources),))],
        flops * HA,
        6_000_000,
        (pos, *sources),
    )
    sources = (all_b, *eff_b, sums, scales, dots, rows)
    (both,) = call(
        features_b_kernel,
        (out(tokens, 2 * width + BLK),),
        [smem()] + [anywhere] * len(sources),
        [pltpu.VMEM((tokens, width), f32)] * 2
        + [pltpu.VMEM(v.shape, v.dtype) for v in sources]
        + [pltpu.SemaphoreType.DMA((len(sources),))],
        flops * HB,
        8_000_000,
        (pos, *sources),
    )
    got = lax.all_to_all(both.reshape(-1, mine, both.shape[1]), "row", 0, 0, tiled=True)
    gate_wgrad, up_wgrad, down_wgrad = call(
        weights_kernel,
        (shape(w_gate), shape(w_up), shape(w_down)),
        [smem()] * 4 + [vmem()] + [anywhere] * 3,
        [left, left]
        + [pltpu.VMEM(v.shape, bf16) for v in (rows, all_a, all_b)]
        + [pltpu.SemaphoreType.DMA((3,))],
        flops * (HA + HB),
        9_000_000,
        (pos, mask_gate, mask_up, mask_down, gain, rows, all_a, all_b),
    )
    layer_out, input_grad, gain_grad = call(
        final_kernel,
        (shape(layer_input), shape(out_grad), shape(gain)),
        [vmem()] * 5,
        [],
        0,
        1_000_000,
        (got, layer_input, out_grad, gain, own_scale),
        mib=16,
    )
    return (layer_out, input_grad, gain_grad[0], gate_wgrad, up_wgrad, down_wgrad)


def solution(mesh):
    torus = Mesh(mesh.devices.reshape(mesh.shape["row"], NZ, NX), ALL)
    placed = (
        P("row", COL),
        P(COL),
        P(COL, "row"),
        P(COL, "row"),
        P("row", COL),
        P(COL, "row"),
        P(COL, "row"),
        P("row", COL),
        P("row", COL),
    )
    return jax.shard_map(
        shards,
        mesh=torus,
        in_specs=placed,
        out_specs=(
            P("row", COL),
            P("row", COL),
            P(COL),
            P(COL, "row"),
            P(COL, "row"),
            P("row", COL),
        ),
        check_vma=False,
    )
```

```python
import functools

import jax
import jax.numpy as jnp
from jax import lax
from jax.experimental import pallas as pl
from jax.experimental.pallas import tpu as pltpu
from jax.sharding import Mesh
from jax.sharding import PartitionSpec as P

D = 8192
BLK = 128
NZ, NX = 8, 4
HA, HB = 768, 1024
COL = ("col_0", "col_1")
ALL = ("row", "col_0", "col_1")
norm_eps = 1e-05

f32 = jnp.float32
bf16 = jnp.bfloat16


def vmem():
    return pl.BlockSpec(memory_space=pltpu.VMEM)


def smem():
    return pl.BlockSpec(memory_space=pltpu.SMEM)


def call(kernel, outs, in_specs, scratch, flops, nbytes, args, mib=56, grid=()):
    whole = [pl.BlockSpec(o.shape, lambda *_, n=len(o.shape): (0,) * n) for o in outs]
    return pl.pallas_call(
        kernel,
        out_shape=outs,
        grid=grid,
        in_specs=in_specs,
        out_specs=tuple(whole if grid else [vmem() for _ in outs]),
        scratch_shapes=scratch,
        compiler_params=pltpu.CompilerParams(vmem_limit_bytes=mib * 1024 * 1024),
        cost_estimate=pl.CostEstimate(flops=flops, bytes_accessed=nbytes, transcendentals=0),
    )(*args)


def nn(a, b):
    return jnp.dot(a, b, preferred_element_type=f32)


def nt(a, b):
    return lax.dot_general(a, b, (((1,), (1,)), ((), ())), preferred_element_type=f32)


def tn(a, b):
    return lax.dot_general(a, b, (((0,), (0,)), ((), ())), preferred_element_type=f32)


def parts3(v):
    hi = v.astype(bf16)
    rest = v - hi.astype(f32)
    mid = rest.astype(bf16)
    return hi, mid, (rest - mid.astype(f32)).astype(bf16)


def lane_sum(block, at):
    return sum(block[:, i : i + 1].astype(f32) for i in range(at, at + 3))


def pieces_of_tokens(pos):
    for tz in range(NZ):
        for tx in range(NX):
            j = lax.rem(tx - pos[2] + NX, NX)
            nat = slice(tz * 64 + tx * 16, tz * 64 + tx * 16 + 16)
            in_a = slice((tx * NZ + tz) * 16, (tx * NZ + tz) * 16 + 16)
            in_b = pl.ds(pl.multiple_of(tz * 64 + j * 16, 16), 16)
            yield nat, in_a, in_b


def masks_kernel(mg, mu, md, wg, wu, wd, ag, au, ad, bg, bu, bd):
    for w, m, ea, eb, down in ((wg, mg, ag, bg, 0), (wu, mu, au, bu, 0), (wd, md, ad, bd, 1)):
        for a in range(w.shape[0] // BLK):
            for b in range(w.shape[1] // BLK):
                r, c = slice(a * BLK, (a + 1) * BLK), slice(b * BLK, (b + 1) * BLK)
                v = w[r, c] * m[a, b].astype(f32).astype(bf16)
                at = (a if down else b) * BLK
                to = slice(at % HA, at % HA + BLK) if at < HA else slice(at - HA, at - HA + BLK)
                e = ea if at < HA else eb
                if down:
                    e[to, c] = v
                else:
                    e[r, to] = v


def products(left, tok, eff, part, to, half):
    width = left.shape[1] // 2
    x, g = left[tok, :width], left[tok, width:]
    part[to, :half] = nn(x, eff[0][...]).astype(bf16)
    part[to, half : 2 * half] = nn(x, eff[1][...]).astype(bf16)
    part[to, 2 * half : 3 * half] = nt(g, eff[2][...]).astype(bf16)


def scaled(rows, nat, gain):
    width = gain.shape[1]
    return (rows[nat, :width].astype(f32) * gain[...]).astype(bf16)


def square_sums(rows, nat, width):
    sq = jnp.square(rows[nat, :width].astype(f32))
    return (sq[:, :BLK] + sq[:, BLK:]).astype(bf16)


def part_a_kernel(rows, gain, eg, eu, ed, part, left):
    width = gain.shape[1]
    for tz in range(NZ):
        for tx in range(NX):
            nat = slice(tz * 64 + tx * 16, tz * 64 + tx * 16 + 16)
            to = slice((tx * NZ + tz) * 16, (tx * NZ + tz) * 16 + 16)
            left[to, :width] = scaled(rows, nat, gain)
            left[to, width:] = rows[nat, width:]
    for t in range(0, left.shape[0], 512):
        products(left, slice(t, t + 512), (eg, eu, ed), part, slice(t, t + 512), HA)


def part_b_kernel(pos, rows, gain, eg, eu, ed, part, left):
    width = gain.shape[1]
    for nat, _, to in pieces_of_tokens(pos):
        left[to, :width] = scaled(rows, nat, gain)
        left[to, width:] = rows[nat, width:]
        part[to, 3 * HB :] = square_sums(rows, nat, width)
    for t in range(0, left.shape[0], 512):
        products(left, slice(t, t + 512), (eg, eu, ed), part, slice(t, t + 512), HB)


def split_kernel(mine, after, *outs):
    for j, out in enumerate(outs, 1):
        out[...] = mine[j * 16 : j * 16 + 16, :]


def join_kernel(*refs):
    *pieces, _, out = refs
    for j, v in enumerate(pieces):
        out[j * 16 : j * 16 + 16, :] = v[...]


def hidden_grads(sums, half, scale, to_act, to_gate, to_up):
    dots = jnp.zeros((16, BLK), f32)
    for c in range(0, half, BLK):
        gate = sums(c) * scale
        up = sums(half + c) * scale
        act_grad = sums(2 * half + c)
        sig = jax.nn.sigmoid(gate)
        act = (gate * sig * up).astype(bf16)
        gate_grad = (act_grad * up * sig * (1.0 + gate * (1.0 - sig))).astype(bf16)
        up_grad = (act_grad * gate * sig).astype(bf16)
        to_act(c, act)
        to_gate(c, gate_grad)
        to_up(c, up_grad)
        dots += gate_grad.astype(f32) * gate + up_grad.astype(f32) * up
    return dots


def grads_b_kernel(part, j1, j2, j3, send, scale, dots):
    def sums(c):
        at = slice(c, c + BLK)
        v = part[:16, at].astype(f32)
        for j in (j1, j2, j3):
            v = v + j[:, at].astype(f32)
        return v

    def store(at):
        def put(c, v):
            send[:, at + c : at + c + BLK] = v

        return put

    squares = jnp.sum(sums(3 * HB), axis=1, keepdims=True)
    sc = lax.rsqrt(squares / D + norm_eps)
    scale[...] = jnp.broadcast_to(sc, scale.shape)
    dots[...] = hidden_grads(sums, HB, sc, store(0), store(HB), store(2 * HB))


def grads_a_kernel(got, scale, dots_b, copies):
    def sums(c):
        return jnp.sum(got[:, :, c : c + BLK].astype(f32), axis=0)

    def store(at):
        def put(c, v):
            for n in range(NZ):
                copies[n, :, at + c : at + c + BLK] = v

        return put

    sc = scale[:, :1]
    dots = dots_b[...] + hidden_grads(sums, HA, sc, store(0), store(HA), store(2 * HA))
    lane = lax.broadcasted_iota(jnp.int32, (16, BLK), 1)
    extra = jnp.zeros((16, BLK), f32)
    for i, v in enumerate(parts3(sc) + parts3(jnp.sum(dots, axis=1, keepdims=True))):
        extra = jnp.where(lane == i, v.astype(f32), extra)
    store(3 * HA)(0, extra.astype(bf16))


def fetch(sources, targets, sems):
    copies = []
    for i, (a, b) in enumerate(zip(sources, targets)):
        copies.append(pltpu.make_async_copy(a, b, sems.at[i]))
        copies[-1].start()
    return copies


def copies_kernel(x, grad, out):
    width = x.shape[1]
    for r in range(out.shape[0]):
        out[r, :, :width] = x[...]
        out[r, :, width:] = grad[...]


def features(hid, half, eg, eu, ed, down, norm):
    down[...] = nn(hid[:, :half], ed[...])
    norm[...] = nt(hid[:, half : 2 * half], eg[...]) + nt(hid[:, 2 * half : 3 * half], eu[...])


def features_a_kernel(pos, *rest):
    n = 4
    sums, scales, dots, own_scale, da, na = rest[n : n + 6]
    held, sems = rest[n + 6 : -1], rest[-1]
    for c in fetch(rest[:n], held, sems):
        c.wait()
    ga, eg, eu, ed = held
    width = eg.shape[0]
    features(ga, HA, eg, eu, ed, da, na)
    lane = lax.broadcasted_iota(jnp.int32, (16, BLK), 1)
    for nat, in_a, _ in pieces_of_tokens(pos):
        sums[nat, :width] = da[in_a, :]
        sums[nat, width:] = na[in_a, :]
        extra = ga[in_a, 3 * HA :].astype(f32)
        scales[nat, :] = jnp.broadcast_to(lane_sum(extra, 0), (16, BLK))
        dots[nat, :] = jnp.where(lane < 3, pltpu.roll(extra, BLK - 3, 1), 0.0).astype(bf16)
    for tx in range(NX):
        at = pl.ds(pl.multiple_of(tx * 128 + pos[0] * 16, 16), 16)
        s = lane_sum(ga[at, 3 * HA :], 0)
        own_scale[tx * 16 : tx * 16 + 16, :] = jnp.broadcast_to(s, (16, BLK))


def features_b_kernel(pos, *rest):
    n = 8
    both, db, nb = rest[n : n + 3]
    held, sems = rest[n + 3 : -1], rest[-1]
    copies = fetch(rest[:n], held, sems)
    for c in copies[:4]:
        c.wait()
    gb, eg, eu, ed, sums, scales, dots, rows = held
    width = eg.shape[0]
    features(gb, HB, eg, eu, ed, db, nb)
    for c in copies[4:]:
        c.wait()
    total = jnp.zeros((16, width), f32)
    for nat, _, in_b in pieces_of_tokens(pos):
        both[nat, :width] = (sums[nat, :width] + db[in_b, :]).astype(bf16)
        grad = sums[nat, width:] + nb[in_b, :]
        both[nat, width : 2 * width] = grad.astype(bf16)
        total += grad * rows[nat, :width].astype(f32) * scales[nat, :1]
    gain_row = jnp.sum(total, axis=0, keepdims=True)
    lane = lax.broadcasted_iota(jnp.int32, (64, BLK), 1)
    line = lax.broadcasted_iota(jnp.int32, (64, BLK), 0)
    shared = jnp.zeros((64, BLK), f32)
    for c in range(width // 64):
        half_row = gain_row[:, (c // 2) * BLK : (c // 2 + 1) * BLK]
        picked = jnp.where(lane == line + 64 * (c % 2), half_row, 0.0)
        for i, v in enumerate(parts3(jnp.sum(picked, axis=1, keepdims=True))):
            shared = jnp.where(lane == 3 + 3 * c + i, v.astype(f32), shared)
    shared = shared.astype(bf16)
    for tz in range(NZ):
        nat = slice(tz * 64, tz * 64 + 64)
        both[nat, 2 * width :] = shared + dots[nat, :]


def weights_kernel(pos, mg, mu, md, gain, *rest):
    sources, (out_g, out_u, out_d, la, lb, rows, ga, gb, sems) = rest[:3], rest[3:]
    copies = fetch(sources, (rows, ga, gb), sems)
    copies[0].wait()
    copies[1].wait()
    width = gain.shape[1]
    for nat, in_a, in_b in pieces_of_tokens(pos):
        scale = lane_sum(ga[in_a, 3 * HA :], 0)
        x = (rows[nat, :width].astype(f32) * scale * gain[...]).astype(bf16)
        g = rows[nat, width:]
        la[in_a, :width] = x
        lb[in_b, :width] = x
        la[in_a, width:] = g
        lb[in_b, width:] = g
    for hid, left, at, half in ((ga, la, 0, HA), (gb, lb, HA, HB)):
        if at:
            copies[2].wait()
        normed, grad = left[:, :width], left[:, width:]
        for c in range(0, half, BLK):
            b = (at + c) // BLK
            gw = tn(normed, hid[:, half + c : half + c + BLK])
            uw = tn(normed, hid[:, 2 * half + c : 2 * half + c + BLK])
            dw = tn(hid[:, c : c + BLK], grad)
            to = slice(at + c, at + c + BLK)
            for a in range(width // BLK):
                r = slice(a * BLK, (a + 1) * BLK)
                out_g[r, to] = (gw[r, :] * mg[a, b].astype(f32)).astype(bf16)
                out_u[r, to] = (uw[r, :] * mu[a, b].astype(f32)).astype(bf16)
                out_d[to, r] = (dw[:, r] * md[b, a].astype(f32)).astype(bf16)


def final_kernel(got, x, grad, gain, scale, layer_out, input_grad, gain_grad):
    width = gain.shape[1]
    s = got[0].astype(f32)
    for r in range(1, got.shape[0]):
        s = s + got[r].astype(f32)
    xf = x[...].astype(f32)
    layer_out[...] = (xf + s[:, :width]).astype(bf16)
    extra = s[:, 2 * width :]
    dots = lane_sum(extra, 0)
    sc = scale[:, :1]
    input_grad[...] = (
        grad[...].astype(f32)
        + sc * gain[...] * s[:, width : 2 * width]
        - xf * sc * sc * (dots / D)
    ).astype(bf16)
    lane = lax.broadcasted_iota(jnp.int32, (64, BLK), 1)
    line = lax.broadcasted_iota(jnp.int32, (64, BLK), 0)
    for h in range(width // BLK):
        spread = jnp.where(
            lane < 64,
            jnp.where(lane == line, lane_sum(extra, 3 + 6 * h), 0.0),
            jnp.where(lane == line + 64, lane_sum(extra, 6 + 6 * h), 0.0),
        )
        gain_grad[:, h * BLK : (h + 1) * BLK] = jnp.sum(spread, axis=0, keepdims=True)


def send(v, axis, step):
    n = lax.axis_size(axis)
    return lax.ppermute(v, axis, [(i, (i + step) % n) for i in range(n)])


def from_everyone(shard, axis):
    copies = jnp.broadcast_to(shard, (lax.axis_size(axis), *shard.shape))
    got = lax.all_to_all(copies, axis, split_axis=0, concat_axis=0, tiled=True)
    return got.reshape(-1, shard.shape[-1])


def shape(v):
    return jax.ShapeDtypeStruct(v.shape, v.dtype)


def shards(layer_input, norm_gain, w_gate, w_up, w_down, mask_gate, mask_up, mask_down, out_grad):
    pos = jnp.stack([lax.axis_index(a) for a in ALL]).astype(jnp.int32)
    gain = norm_gain[None, :]
    mine, width = layer_input.shape
    n_rows = lax.axis_size("row")
    tokens = n_rows * mine
    flops = 2 * tokens * width * 3
    a_cols, b_cols = 3 * HA, 3 * HB + BLK

    def out(*dims, dtype=bf16):
        return jax.ShapeDtypeStruct(dims, dtype)

    (first,) = call(
        copies_kernel,
        (out(n_rows, mine, 2 * width),),
        [vmem()] * 2,
        [],
        0,
        600_000,
        (layer_input, out_grad),
        mib=56,
    )
    rows = lax.all_to_all(first, "row", 0, 0, tiled=True).reshape(tokens, -1)
    eff = call(
        masks_kernel,
        (*[out(width, HA)] * 2, out(HA, width), *[out(width, HB)] * 2, out(HB, width)),
        [smem()] * 3 + [vmem()] * 3,
        [],
        0,
        6_000_000,
        (mask_gate, mask_up, mask_down, w_gate, w_up, w_down),
        mib=56,
    )
    eff_a, eff_b = eff[:3], eff[3:]
    left = pltpu.VMEM((tokens, 2 * width), bf16)
    (part_a,) = call(
        part_a_kernel,
        (out(tokens, a_cols),),
        [vmem()] * 5,
        [left],
        flops * HA,
        4_000_000,
        (rows, gain, *eff_a),
        mib=56,
    )
    (part_b,) = call(
        part_b_kernel,
        (out(tokens, b_cols),),
        [smem()] + [vmem()] * 5,
        [left],
        flops * HB,
        5_000_000,
        (pos, rows, gain, *eff_b),
        mib=56,
    )
    got_a = lax.all_to_all(part_a.reshape(NX, -1, a_cols), "col_1", 0, 0, tiled=True)
    mine_b = lax.psum_scatter(part_b, "col_0", scatter_dimension=0, tiled=True)
    sum_a = jnp.sum(got_a.astype(f32), axis=0).astype(bf16).reshape(NZ, -1, a_cols)
    others = call(
        split_kernel,
        tuple([out(16, b_cols)] * (NX - 1)),
        [vmem(), pl.BlockSpec(memory_space=pl.ANY)],
        [],
        0,
        600_000,
        (mine_b, sum_a),
        mib=16,
    )
    got_b = [send(others[j - 1], "col_1", j) for j in (1, 3, 2)]
    got_a = lax.all_to_all(sum_a, "col_0", 0, 0, tiled=True)
    send_b, scale, dots_b = call(
        grads_b_kernel,
        (out(16, 3 * HB), out(16, BLK, dtype=f32), out(16, BLK, dtype=f32)),
        [vmem()] * 4,
        [],
        0,
        600_000,
        (mine_b, *got_b),
        mib=16,
    )
    (copies_a,) = call(
        grads_a_kernel,
        (out(NZ, 16, a_cols + BLK),),
        [vmem()] * 3,
        [],
        0,
        1_500_000,
        (got_a, scale, dots_b),
        mib=16,
    )
    near = [send_b] + [send(send_b, "col_1", -j) for j in (1, 3, 2)]
    near = [near[0], near[1], near[3], near[2]]
    (near,) = call(
        join_kernel,
        (out(NX * 16, 3 * HB),),
        [vmem()] * NX + [pl.BlockSpec(memory_space=pl.ANY)],
        [],
        0,
        600_000,
        (*near, got_a),
        mib=16,
    )
    all_b = lax.all_gather(near, "col_0", axis=0, tiled=True)
    all_a = lax.all_to_all(copies_a, "col_0", 0, 0, tiled=True).reshape(-1, a_cols + BLK)
    all_a = from_everyone(all_a, "col_1")

    anywhere = pl.BlockSpec(memory_space=pl.ANY)
    f_shape = functools.partial(out, dtype=f32)
    sources = (all_a, *eff_a)
    sums, scales, dots, own_scale = call(
        features_a_kernel,
        (f_shape(tokens, 2 * width), f_shape(tokens, BLK), out(tokens, BLK), f_shape(mine, BLK)),
        [smem()] + [anywhere] * len(sources),
        [pltpu.VMEM((tokens, width), f32)] * 2
        + [pltpu.VMEM(v.shape, v.dtype) for v in sources]
        + [pltpu.SemaphoreType.DMA((len(sources),))],
        flops * HA,
        6_000_000,
        (pos, *sources),
    )
    sources = (all_b, *eff_b, sums, scales, dots, rows)
    (both,) = call(
        features_b_kernel,
        (out(tokens, 2 * width + BLK),),
        [smem()] + [anywhere] * len(sources),
        [pltpu.VMEM((tokens, width), f32)] * 2
        + [pltpu.VMEM(v.shape, v.dtype) for v in sources]
        + [pltpu.SemaphoreType.DMA((len(sources),))],
        flops * HB,
        8_000_000,
        (pos, *sources),
    )
    got = lax.all_to_all(both.reshape(-1, mine, both.shape[1]), "row", 0, 0, tiled=True)
    gate_wgrad, up_wgrad, down_wgrad = call(
        weights_kernel,
        (shape(w_gate), shape(w_up), shape(w_down)),
        [smem()] * 4 + [vmem()] + [anywhere] * 3,
        [left, left]
        + [pltpu.VMEM(v.shape, bf16) for v in (rows, all_a, all_b)]
        + [pltpu.SemaphoreType.DMA((3,))],
        flops * (HA + HB),
        9_000_000,
        (pos, mask_gate, mask_up, mask_down, gain, rows, all_a, all_b),
    )
    layer_out, input_grad, gain_grad = call(
        final_kernel,
        (shape(layer_input), shape(out_grad), shape(gain)),
        [vmem()] * 5,
        [],
        0,
        1_000_000,
        (got, layer_input, out_grad, gain, own_scale),
        mib=16,
    )
    return (layer_out, input_grad, gain_grad[0], gate_wgrad, up_wgrad, down_wgrad)


def solution(mesh):
    torus = Mesh(mesh.devices.reshape(mesh.shape["row"], NZ, NX), ALL)
    placed = (
        P("row", COL),
        P(COL),
        P(COL, "row"),
        P(COL, "row"),
        P("row", COL),
        P(COL, "row"),
        P(COL, "row"),
        P("row", COL),
        P("row", COL),
    )
    return jax.shard_map(
        shards,
        mesh=torus,
        in_specs=placed,
        out_specs=(
            P("row", COL),
            P("row", COL),
            P(COL),
            P(COL, "row"),
            P(COL, "row"),
            P("row", COL),
        ),
        check_vma=False,
    )
```

```python
import functools

import jax
import jax.numpy as jnp
from jax import lax
from jax.experimental import pallas as pl
from jax.experimental.pallas import tpu as pltpu
from jax.sharding import Mesh
from jax.sharding import PartitionSpec as P

D = 8192
BLK = 128
NZ, NX = 8, 4
HA, HB = 768, 1024
COL = ("col_0", "col_1")
ALL = ("row", "col_0", "col_1")
norm_eps = 1e-05

f32 = jnp.float32
bf16 = jnp.bfloat16


def vmem():
    return pl.BlockSpec(memory_space=pltpu.VMEM)


def smem():
    return pl.BlockSpec(memory_space=pltpu.SMEM)


def call(kernel, outs, in_specs, scratch, flops, nbytes, args, mib=56, grid=()):
    whole = [pl.BlockSpec(o.shape, lambda *_, n=len(o.shape): (0,) * n) for o in outs]
    return pl.pallas_call(
        kernel,
        out_shape=outs,
        grid=grid,
        in_specs=in_specs,
        out_specs=tuple(whole if grid else [vmem() for _ in outs]),
        scratch_shapes=scratch,
        compiler_params=pltpu.CompilerParams(vmem_limit_bytes=mib * 1024 * 1024),
        cost_estimate=pl.CostEstimate(flops=flops, bytes_accessed=nbytes, transcendentals=0),
    )(*args)


def nn(a, b):
    return jnp.dot(a, b, preferred_element_type=f32)


def nt(a, b):
    return lax.dot_general(a, b, (((1,), (1,)), ((), ())), preferred_element_type=f32)


def tn(a, b):
    return lax.dot_general(a, b, (((0,), (0,)), ((), ())), preferred_element_type=f32)


def parts3(v):
    hi = v.astype(bf16)
    rest = v - hi.astype(f32)
    mid = rest.astype(bf16)
    return hi, mid, (rest - mid.astype(f32)).astype(bf16)


def lane_sum(block, at):
    return sum(block[:, i : i + 1].astype(f32) for i in range(at, at + 3))


def pieces_of_tokens(pos):
    for tz in range(NZ):
        for tx in range(NX):
            j = lax.rem(tx - pos[2] + NX, NX)
            nat = slice(tz * 64 + tx * 16, tz * 64 + tx * 16 + 16)
            in_a = slice((tx * NZ + tz) * 16, (tx * NZ + tz) * 16 + 16)
            in_b = pl.ds(pl.multiple_of(tz * 64 + j * 16, 16), 16)
            yield nat, in_a, in_b


def masks_kernel(mg, mu, md, wg, wu, wd, ag, au, ad, bg, bu, bd):
    for w, m, ea, eb, down in ((wg, mg, ag, bg, 0), (wu, mu, au, bu, 0), (wd, md, ad, bd, 1)):
        for a in range(w.shape[0] // BLK):
            for b in range(w.shape[1] // BLK):
                r, c = slice(a * BLK, (a + 1) * BLK), slice(b * BLK, (b + 1) * BLK)
                v = w[r, c] * m[a, b].astype(f32).astype(bf16)
                at = (a if down else b) * BLK
                to = slice(at % HA, at % HA + BLK) if at < HA else slice(at - HA, at - HA + BLK)
                e = ea if at < HA else eb
                if down:
                    e[to, c] = v
                else:
                    e[r, to] = v


def products(left, tok, eff, part, to, half):
    width = left.shape[1] // 2
    x, g = left[tok, :width], left[tok, width:]
    part[to, :half] = nn(x, eff[0][...]).astype(bf16)
    part[to, half : 2 * half] = nn(x, eff[1][...]).astype(bf16)
    part[to, 2 * half : 3 * half] = nt(g, eff[2][...]).astype(bf16)


def scaled(rows, nat, gain):
    width = gain.shape[1]
    return (rows[nat, :width].astype(f32) * gain[...]).astype(bf16)


def square_sums(rows, nat, width):
    sq = jnp.square(rows[nat, :width].astype(f32))
    return (sq[:, :BLK] + sq[:, BLK:]).astype(bf16)


def part_a_kernel(rows, gain, eg, eu, ed, part, left):
    width = gain.shape[1]
    for tz in range(NZ):
        for tx in range(NX):
            nat = slice(tz * 64 + tx * 16, tz * 64 + tx * 16 + 16)
            to = slice((tx * NZ + tz) * 16, (tx * NZ + tz) * 16 + 16)
            left[to, :width] = scaled(rows, nat, gain)
            left[to, width:] = rows[nat, width:]
    for t in range(0, left.shape[0], 512):
        products(left, slice(t, t + 512), (eg, eu, ed), part, slice(t, t + 512), HA)


def part_b_kernel(pos, rows, gain, eg, eu, ed, part, left):
    width = gain.shape[1]
    for nat, _, to in pieces_of_tokens(pos):
        left[to, :width] = scaled(rows, nat, gain)
        left[to, width:] = rows[nat, width:]
        part[to, 3 * HB :] = square_sums(rows, nat, width)
    for t in range(0, left.shape[0], 512):
        products(left, slice(t, t + 512), (eg, eu, ed), part, slice(t, t + 512), HB)


def sum_kernel(got, out):
    for r in range(NZ):
        at = slice(r * 16, r * 16 + 16)
        total = got[0, at, :].astype(f32)
        for j in range(1, NX):
            total = total + got[j, at, :].astype(f32)
        out[r] = total.astype(bf16)


def split_kernel(mine, after, *outs):
    for j, out in enumerate(outs, 1):
        out[...] = mine[j * 16 : j * 16 + 16, :]


def join_kernel(*refs):
    *pieces, _, out = refs
    for j, v in enumerate(pieces):
        out[j * 16 : j * 16 + 16, :] = v[...]


def hidden_grads(sums, half, scale, to_act, to_gate, to_up):
    dots = jnp.zeros((16, BLK), f32)
    for c in range(0, half, BLK):
        gate = sums(c) * scale
        up = sums(half + c) * scale
        act_grad = sums(2 * half + c)
        sig = jax.nn.sigmoid(gate)
        act = (gate * sig * up).astype(bf16)
        gate_grad = (act_grad * up * sig * (1.0 + gate * (1.0 - sig))).astype(bf16)
        up_grad = (act_grad * gate * sig).astype(bf16)
        to_act(c, act)
        to_gate(c, gate_grad)
        to_up(c, up_grad)
        dots += gate_grad.astype(f32) * gate + up_grad.astype(f32) * up
    return dots


def grads_b_kernel(part, j1, j2, j3, send, scale, dots):
    def sums(c):
        at = slice(c, c + BLK)
        v = part[:16, at].astype(f32)
        for j in (j1, j2, j3):
            v = v + j[:, at].astype(f32)
        return v

    def store(at):
        def put(c, v):
            send[:, at + c : at + c + BLK] = v

        return put

    squares = jnp.sum(sums(3 * HB), axis=1, keepdims=True)
    sc = lax.rsqrt(squares / D + norm_eps)
    scale[...] = jnp.broadcast_to(sc, scale.shape)
    dots[...] = hidden_grads(sums, HB, sc, store(0), store(HB), store(2 * HB))


def grads_a_kernel(got, scale, dots_b, copies):
    def sums(c):
        return jnp.sum(got[:, :, c : c + BLK].astype(f32), axis=0)

    def store(at):
        def put(c, v):
            for n in range(NZ):
                copies[n, :, at + c : at + c + BLK] = v

        return put

    sc = scale[:, :1]
    dots = dots_b[...] + hidden_grads(sums, HA, sc, store(0), store(HA), store(2 * HA))
    lane = lax.broadcasted_iota(jnp.int32, (16, BLK), 1)
    extra = jnp.zeros((16, BLK), f32)
    for i, v in enumerate(parts3(sc) + parts3(jnp.sum(dots, axis=1, keepdims=True))):
        extra = jnp.where(lane == i, v.astype(f32), extra)
    store(3 * HA)(0, extra.astype(bf16))


def fetch(sources, targets, sems):
    copies = []
    for i, (a, b) in enumerate(zip(sources, targets)):
        copies.append(pltpu.make_async_copy(a, b, sems.at[i]))
        copies[-1].start()
    return copies


def copies_kernel(x, grad, out):
    width = x.shape[1]
    for r in range(out.shape[0]):
        out[r, :, :width] = x[...]
        out[r, :, width:] = grad[...]


def features(hid, half, eg, eu, ed, down, norm):
    down[...] = nn(hid[:, :half], ed[...])
    norm[...] = nt(hid[:, half : 2 * half], eg[...]) + nt(hid[:, 2 * half : 3 * half], eu[...])


def features_a_kernel(pos, *rest):
    n = 4
    sums, scales, dots, own_scale, da, na = rest[n : n + 6]
    held, sems = rest[n + 6 : -1], rest[-1]
    for c in fetch(rest[:n], held, sems):
        c.wait()
    ga, eg, eu, ed = held
    width = eg.shape[0]
    features(ga, HA, eg, eu, ed, da, na)
    lane = lax.broadcasted_iota(jnp.int32, (16, BLK), 1)
    for nat, in_a, _ in pieces_of_tokens(pos):
        sums[nat, :width] = da[in_a, :]
        sums[nat, width:] = na[in_a, :]
        extra = ga[in_a, 3 * HA :].astype(f32)
        scales[nat, :] = jnp.broadcast_to(lane_sum(extra, 0), (16, BLK))
        dots[nat, :] = jnp.where(lane < 3, pltpu.roll(extra, BLK - 3, 1), 0.0).astype(bf16)
    for tx in range(NX):
        at = pl.ds(pl.multiple_of(tx * 128 + pos[0] * 16, 16), 16)
        s = lane_sum(ga[at, 3 * HA :], 0)
        own_scale[tx * 16 : tx * 16 + 16, :] = jnp.broadcast_to(s, (16, BLK))


def features_b_kernel(pos, *rest):
    n = 8
    both, db, nb = rest[n : n + 3]
    held, sems = rest[n + 3 : -1], rest[-1]
    copies = fetch(rest[:n], held, sems)
    for c in copies[:4]:
        c.wait()
    gb, eg, eu, ed, sums, scales, dots, rows = held
    width = eg.shape[0]
    features(gb, HB, eg, eu, ed, db, nb)
    for c in copies[4:]:
        c.wait()
    total = jnp.zeros((16, width), f32)
    for nat, _, in_b in pieces_of_tokens(pos):
        both[nat, :width] = (sums[nat, :width] + db[in_b, :]).astype(bf16)
        grad = sums[nat, width:] + nb[in_b, :]
        both[nat, width : 2 * width] = grad.astype(bf16)
        total += grad * rows[nat, :width].astype(f32) * scales[nat, :1]
    gain_row = jnp.sum(total, axis=0, keepdims=True)
    lane = lax.broadcasted_iota(jnp.int32, (64, BLK), 1)
    line = lax.broadcasted_iota(jnp.int32, (64, BLK), 0)
    shared = jnp.zeros((64, BLK), f32)
    for c in range(width // 64):
        half_row = gain_row[:, (c // 2) * BLK : (c // 2 + 1) * BLK]
        picked = jnp.where(lane == line + 64 * (c % 2), half_row, 0.0)
        for i, v in enumerate(parts3(jnp.sum(picked, axis=1, keepdims=True))):
            shared = jnp.where(lane == 3 + 3 * c + i, v.astype(f32), shared)
    shared = shared.astype(bf16)
    for tz in range(NZ):
        nat = slice(tz * 64, tz * 64 + 64)
        both[nat, 2 * width :] = shared + dots[nat, :]


def weights_kernel(pos, mg, mu, md, gain, *rest):
    sources, (out_g, out_u, out_d, la, lb, rows, ga, gb, sems) = rest[:3], rest[3:]
    copies = fetch(sources, (rows, ga, gb), sems)
    copies[0].wait()
    copies[1].wait()
    width = gain.shape[1]
    for nat, in_a, in_b in pieces_of_tokens(pos):
        scale = lane_sum(ga[in_a, 3 * HA :], 0)
        x = (rows[nat, :width].astype(f32) * scale * gain[...]).astype(bf16)
        g = rows[nat, width:]
        la[in_a, :width] = x
        lb[in_b, :width] = x
        la[in_a, width:] = g
        lb[in_b, width:] = g
    for hid, left, at, half in ((ga, la, 0, HA), (gb, lb, HA, HB)):
        if at:
            copies[2].wait()
        normed, grad = left[:, :width], left[:, width:]
        for c in range(0, half, BLK):
            b = (at + c) // BLK
            gw = tn(normed, hid[:, half + c : half + c + BLK])
            uw = tn(normed, hid[:, 2 * half + c : 2 * half + c + BLK])
            dw = tn(hid[:, c : c + BLK], grad)
            to = slice(at + c, at + c + BLK)
            for a in range(width // BLK):
                r = slice(a * BLK, (a + 1) * BLK)
                out_g[r, to] = (gw[r, :] * mg[a, b].astype(f32)).astype(bf16)
                out_u[r, to] = (uw[r, :] * mu[a, b].astype(f32)).astype(bf16)
                out_d[to, r] = (dw[:, r] * md[b, a].astype(f32)).astype(bf16)


def final_kernel(got, x, grad, gain, scale, layer_out, input_grad, gain_grad):
    width = gain.shape[1]
    s = got[0].astype(f32)
    for r in range(1, got.shape[0]):
        s = s + got[r].astype(f32)
    xf = x[...].astype(f32)
    layer_out[...] = (xf + s[:, :width]).astype(bf16)
    extra = s[:, 2 * width :]
    dots = lane_sum(extra, 0)
    sc = scale[:, :1]
    input_grad[...] = (
        grad[...].astype(f32)
        + sc * gain[...] * s[:, width : 2 * width]
        - xf * sc * sc * (dots / D)
    ).astype(bf16)
    lane = lax.broadcasted_iota(jnp.int32, (64, BLK), 1)
    line = lax.broadcasted_iota(jnp.int32, (64, BLK), 0)
    for h in range(width // BLK):
        spread = jnp.where(
            lane < 64,
            jnp.where(lane == line, lane_sum(extra, 3 + 6 * h), 0.0),
            jnp.where(lane == line + 64, lane_sum(extra, 6 + 6 * h), 0.0),
        )
        gain_grad[:, h * BLK : (h + 1) * BLK] = jnp.sum(spread, axis=0, keepdims=True)


def send(v, axis, step):
    n = lax.axis_size(axis)
    return lax.ppermute(v, axis, [(i, (i + step) % n) for i in range(n)])


def from_everyone(shard, axis):
    copies = jnp.broadcast_to(shard, (lax.axis_size(axis), *shard.shape))
    got = lax.all_to_all(copies, axis, split_axis=0, concat_axis=0, tiled=True)
    return got.reshape(-1, shard.shape[-1])


def shape(v):
    return jax.ShapeDtypeStruct(v.shape, v.dtype)


def shards(layer_input, norm_gain, w_gate, w_up, w_down, mask_gate, mask_up, mask_down, out_grad):
    pos = jnp.stack([lax.axis_index(a) for a in ALL]).astype(jnp.int32)
    gain = norm_gain[None, :]
    mine, width = layer_input.shape
    n_rows = lax.axis_size("row")
    tokens = n_rows * mine
    flops = 2 * tokens * width * 3
    a_cols, b_cols = 3 * HA, 3 * HB + BLK

    def out(*dims, dtype=bf16):
        return jax.ShapeDtypeStruct(dims, dtype)

    (first,) = call(
        copies_kernel,
        (out(n_rows, mine, 2 * width),),
        [vmem()] * 2,
        [],
        0,
        600_000,
        (layer_input, out_grad),
        mib=56,
    )
    rows = lax.all_to_all(first, "row", 0, 0, tiled=True).reshape(tokens, -1)
    eff = call(
        masks_kernel,
        (*[out(width, HA)] * 2, out(HA, width), *[out(width, HB)] * 2, out(HB, width)),
        [smem()] * 3 + [vmem()] * 3,
        [],
        0,
        6_000_000,
        (mask_gate, mask_up, mask_down, w_gate, w_up, w_down),
        mib=56,
    )
    eff_a, eff_b = eff[:3], eff[3:]
    left = pltpu.VMEM((tokens, 2 * width), bf16)
    (part_a,) = call(
        part_a_kernel,
        (out(tokens, a_cols),),
        [vmem()] * 5,
        [left],
        flops * HA,
        4_000_000,
        (rows, gain, *eff_a),
        mib=56,
    )
    (part_b,) = call(
        part_b_kernel,
        (out(tokens, b_cols),),
        [smem()] + [vmem()] * 5,
        [left],
        flops * HB,
        5_000_000,
        (pos, rows, gain, *eff_b),
        mib=56,
    )
    got_a = lax.all_to_all(part_a.reshape(NX, -1, a_cols), "col_1", 0, 0, tiled=True)
    mine_b = lax.psum_scatter(part_b, "col_0", scatter_dimension=0, tiled=True)
    (sum_a,) = call(
        sum_kernel,
        (out(NZ, 16, a_cols),),
        [vmem()],
        [],
        0,
        2_500_000,
        (got_a,),
        mib=16,
    )
    others = call(
        split_kernel,
        tuple([out(16, b_cols)] * (NX - 1)),
        [vmem(), pl.BlockSpec(memory_space=pl.ANY)],
        [],
        0,
        600_000,
        (mine_b, sum_a),
        mib=16,
    )
    got_b = [send(others[j - 1], "col_1", j) for j in (1, 3, 2)]
    got_a = lax.all_to_all(sum_a, "col_0", 0, 0, tiled=True)
    send_b, scale, dots_b = call(
        grads_b_kernel,
        (out(16, 3 * HB), out(16, BLK, dtype=f32), out(16, BLK, dtype=f32)),
        [vmem()] * 4,
        [],
        0,
        600_000,
        (mine_b, *got_b),
        mib=16,
    )
    (copies_a,) = call(
        grads_a_kernel,
        (out(NZ, 16, a_cols + BLK),),
        [vmem()] * 3,
        [],
        0,
        1_500_000,
        (got_a, scale, dots_b),
        mib=16,
    )
    near = [send_b] + [send(send_b, "col_1", -j) for j in (1, 3, 2)]
    near = [near[0], near[1], near[3], near[2]]
    (near,) = call(
        join_kernel,
        (out(NX * 16, 3 * HB),),
        [vmem()] * NX + [pl.BlockSpec(memory_space=pl.ANY)],
        [],
        0,
        600_000,
        (*near, got_a),
        mib=16,
    )
    all_b = lax.all_gather(near, "col_0", axis=0, tiled=True)
    all_a = lax.all_to_all(copies_a, "col_0", 0, 0, tiled=True).reshape(-1, a_cols + BLK)
    all_a = from_everyone(all_a, "col_1")

    anywhere = pl.BlockSpec(memory_space=pl.ANY)
    f_shape = functools.partial(out, dtype=f32)
    sources = (all_a, *eff_a)
    sums, scales, dots, own_scale = call(
        features_a_kernel,
        (f_shape(tokens, 2 * width), f_shape(tokens, BLK), out(tokens, BLK), f_shape(mine, BLK)),
        [smem()] + [anywhere] * len(sources),
        [pltpu.VMEM((tokens, width), f32)] * 2
        + [pltpu.VMEM(v.shape, v.dtype) for v in sources]
        + [pltpu.SemaphoreType.DMA((len(sources),))],
        flops * HA,
        6_000_000,
        (pos, *sources),
    )
    sources = (all_b, *eff_b, sums, scales, dots, rows)
    (both,) = call(
        features_b_kernel,
        (out(tokens, 2 * width + BLK),),
        [smem()] + [anywhere] * len(sources),
        [pltpu.VMEM((tokens, width), f32)] * 2
        + [pltpu.VMEM(v.shape, v.dtype) for v in sources]
        + [pltpu.SemaphoreType.DMA((len(sources),))],
        flops * HB,
        8_000_000,
        (pos, *sources),
    )
    got = lax.all_to_all(both.reshape(-1, mine, both.shape[1]), "row", 0, 0, tiled=True)
    gate_wgrad, up_wgrad, down_wgrad = call(
        weights_kernel,
        (shape(w_gate), shape(w_up), shape(w_down)),
        [smem()] * 4 + [vmem()] + [anywhere] * 3,
        [left, left]
        + [pltpu.VMEM(v.shape, bf16) for v in (rows, all_a, all_b)]
        + [pltpu.SemaphoreType.DMA((3,))],
        flops * (HA + HB),
        9_000_000,
        (pos, mask_gate, mask_up, mask_down, gain, rows, all_a, all_b),
    )
    layer_out, input_grad, gain_grad = call(
        final_kernel,
        (shape(layer_input), shape(out_grad), shape(gain)),
        [vmem()] * 5,
        [],
        0,
        1_000_000,
        (got, layer_input, out_grad, gain, own_scale),
        mib=16,
    )
    return (layer_out, input_grad, gain_grad[0], gate_wgrad, up_wgrad, down_wgrad)


def solution(mesh):
    torus = Mesh(mesh.devices.reshape(mesh.shape["row"], NZ, NX), ALL)
    placed = (
        P("row", COL),
        P(COL),
        P(COL, "row"),
        P(COL, "row"),
        P("row", COL),
        P(COL, "row"),
        P(COL, "row"),
        P("row", COL),
        P("row", COL),
    )
    return jax.shard_map(
        shards,
        mesh=torus,
        in_specs=placed,
        out_specs=(
            P("row", COL),
            P("row", COL),
            P(COL),
            P(COL, "row"),
            P(COL, "row"),
            P("row", COL),
        ),
        check_vma=False,
    )
```
